256 devices in a mesh: ctx: 32 (over y, z), head: 8 (over x, core).
Axes of the slice: x: 4, y: 4, z: 8, core: 2. Of those that a mesh axis runs over, the one named last changes fastest.
Arguments:
- query: bfloat16 [32768, 5120], P('ctx', 'head'), may hold values from -800 to 800
- key: bfloat16 [32768, 5120], P('ctx', 'head'), may hold values from -800 to 800
- value: bfloat16 [32768, 5120], P('ctx', 'head'), may hold values from -6 to 6
- gain_q: float32 [5120], P('head'), may hold values from 0.1 to 1.9
- gain_k: float32 [5120], P('head'), may hold values from 0.1 to 1.9
- head_kind: int32 [40], replicated, may hold values from 0 to 1, as said below
Outputs:
- attended: bfloat16 [32768, 5120], P('ctx', 'head')
The draws below stay inside these ranges and needn't reach their ends.
Inputs may be any that keep to these rules, and one draw needn't show every extreme that they name: `head_kind`: 1 marks a temporal head, 0 a spatial one; each aligned group of 5 heads (heads 0 to 4, and so on) holds 1 to 3 temporal heads, and in every draw some group holds exactly 1 and some exactly 3.
All inputs are finite; a program needn't handle non-finite values.
Results may differ from the reference program's by a relative error of at most 0.012.
Values may be sent and summed in bfloat16 or wider, within the bound.
A program may use at most 64 MiB of HBM per device.

```python
import math
import jax
import jax.numpy as jnp
from jax import lax

HEADS = 40
HDIM = 128
POS = 2048
GROUP = 5
TLEAST = 1
TMOST = 3
FRAMES = 16
TOKENS = 32768
CHANNELS = 5120


def column_spread(key, strength):
    width_all = HEADS * HDIM
    column_pos = jnp.arange(width_all, dtype=jnp.float32) / (width_all - 1)
    rough = jnp.exp(jax.random.uniform(key, (width_all,), jnp.float32, math.log(0.7), math.log(1.4)))
    return jnp.exp(math.log(strength) * column_pos) * rough


def base_field(key_one, key_two):
    token_count = POS * FRAMES
    width_all = HEADS * HDIM
    spread = column_spread(key_two, 3.0)
    field = jax.random.truncated_normal(key_one, -4.0, 4.0, (token_count, width_all), jnp.float32)
    return field * spread[None, :]


def draw_query(key, part):
    key = jax.random.fold_in(key, 11)
    key_one, key_two = jax.random.split(key, 2)
    field = base_field(key_one, key_two)
    return field.astype(jnp.bfloat16)


def draw_key(key, part):
    key = jax.random.fold_in(key, 23)
    key_one, key_two = jax.random.split(key, 2)
    field = base_field(key_one, key_two)
    return field.astype(jnp.bfloat16)


def draw_head_kind(key, part):
    key = jax.random.fold_in(key, 37)
    key_one, key_two, key_three = jax.random.split(key, 3)
    group_count = HEADS // GROUP
    group_index = jnp.arange(group_count, dtype=jnp.int32)
    counts = jax.random.randint(key_one, (group_count,), TLEAST, TMOST + 1, jnp.int32)
    picked = jax.random.permutation(key_two, group_count)
    counts = jnp.where(group_index == picked[0], TLEAST, jnp.where(group_index == picked[1], TMOST, counts))
    tickets = jax.random.randint(key_three, (group_count, GROUP), 0, 1 << 20, jnp.int32) * GROUP
    tickets = tickets + jnp.arange(GROUP, dtype=jnp.int32)[None, :]
    ranks = jnp.argsort(jnp.argsort(tickets, axis=1), axis=1).astype(jnp.int32)
    return (ranks < counts[:, None]).astype(jnp.int32).reshape(HEADS)


def block_levels(key, extent, cuts, low, largest):
    factor_of = 1.0
    for dim, shards_of in cuts:
        heights = jax.random.uniform(jax.random.fold_in(jax.random.fold_in(key, 6), dim), (shards_of,), jnp.float32, low / len(cuts), largest / len(cuts))
        factor_of = factor_of * jnp.repeat(jnp.exp(heights), extent[dim] // shards_of).reshape((-1,) + (1,) * (len(extent) - 1 - dim))
    return factor_of


def scatter_about(stream_key, dims, scale, limit, shards=(), kind=jnp.bfloat16):
    drawn = jax.random.normal(stream_key, dims, jnp.float32) * scale
    if len(shards) > 0:
        drawn = block_levels(stream_key, dims, shards, -0.22, 0.18) * drawn
    return jnp.clip(drawn, min=-limit, max=limit).astype(kind)


def setup_inputs(seed: int = 0) -> dict:
    keys = jax.random.split(jax.random.key(seed), 7)
    return {
        "query": draw_query(jax.random.fold_in(keys[6], 71), 0),
        "key": draw_key(jax.random.fold_in(keys[6], 71), 0),
        "value": scatter_about(keys[2], (TOKENS, CHANNELS), 1.0, 6.0, ((0, 32), (1, 8))),
        "gain_q": jnp.clip(1.0 + 0.18 * jax.random.normal(keys[3], (CHANNELS,), jnp.float32), 0.1, 1.9),
        "gain_k": jnp.clip(1.0 + 0.18 * jax.random.normal(keys[4], (CHANNELS,), jnp.float32), 0.1, 1.9),
        "head_kind": draw_head_kind(jax.random.fold_in(keys[6], 71), 0),
    }


EPSILON = 1e-06

def normalize(values_in, gain):
    as_float = values_in.astype(jnp.float32)
    row_total = lax.optimization_barrier(jnp.sum(as_float * as_float, axis=1, keepdims=True))
    return (as_float * lax.rsqrt(row_total / (HEADS * HDIM) + EPSILON) * gain).astype(jnp.bfloat16)

def softmax_weights(scores):
    row_top = lax.optimization_barrier(jnp.max(scores, axis=-1, keepdims=True))
    expo_terms = jnp.exp(scores - row_top)
    return (expo_terms / lax.optimization_barrier(jnp.sum(expo_terms, axis=-1, keepdims=True))).astype(jnp.bfloat16)

def reference(query, key, value, gain_q, gain_k, head_kind):
    score_scale = 1.0 / math.sqrt(HDIM)
    frame_count = query.shape[0] // POS
    query_norm = normalize(query, gain_q).reshape(frame_count, POS, HEADS, HDIM)
    key_norm = normalize(key, gain_k).reshape(frame_count, POS, HEADS, HDIM)
    value_four = value.reshape(frame_count, POS, HEADS, HDIM)

    def frame_attend(frame_block):
        query_frame, key_frame, value_frame = frame_block
        scores = jnp.einsum('phd,shd->hps', query_frame.astype(jnp.float32), key_frame.astype(jnp.float32)) * score_scale
        weights = softmax_weights(scores)
        mixed_out = jnp.einsum('hps,shd->phd', weights.astype(jnp.float32), value_frame.astype(jnp.float32))
        return mixed_out.astype(jnp.bfloat16)
    spatial = lax.map(frame_attend, (query_norm, key_norm, value_four))
    temporal_scores = jnp.einsum('fphd,gphd->phfg', query_norm.astype(jnp.float32), key_norm.astype(jnp.float32)) * score_scale
    temporal_weights = softmax_weights(temporal_scores)
    temporal = jnp.einsum('phfg,gphd->fphd', temporal_weights.astype(jnp.float32), value_four.astype(jnp.float32)).astype(jnp.bfloat16)
    temporal_mask = (head_kind == 1)[None, None, :, None]
    attended = jnp.where(temporal_mask, temporal, spatial)
    return attended.reshape(frame_count * POS, HEADS * HDIM)
```

```python
import functools
import math

import jax
import jax.numpy as jnp
from jax import lax
from jax.experimental import pallas as pl
from jax.experimental.pallas import tpu as pltpu
from jax.sharding import PartitionSpec as P

HEADS = 40
HDIM = 128
EPSILON = 1e-06
NT = 3
NS = 4
CHUNK = 128
QROWS = 256
MESH = pl.DeviceIdType.MESH
BF16 = jnp.bfloat16
F32 = jnp.float32


def dot_nt(a, b):
    return lax.dot_general(a, b, (((1,), (1,)), ((), ())), preferred_element_type=F32)


def dot_nn(a, b):
    return lax.dot_general(a, b, (((1,), (0,)), ((), ())), preferred_element_type=F32)


def kernel(
    frames, groups, kind_ref, q_ref, k_ref, v_ref, gq_ref, gk_ref, out_ref,
    vt, qkt, vr, qkr, ot, res, own_k, own_v, par_k, par_v, qs, qn, kn, rq, rk, ss_own, ss_all,
    ss_sems, vt_send, vt_recv, qk_send, qk_recv, ret_send, ret_recv,
    sk_send, sk_recv, sv_send, sv_recv,
):
    tokens, width = q_ref.shape
    heads = width // HDIM
    block = tokens // frames
    chunks = tokens // CHUNK
    score_scale = 1.0 / math.sqrt(HDIM)
    ctx = lax.axis_index("ctx")
    group = lax.axis_index("head")
    frame, half = ctx // 2, ctx % 2
    partner = ctx + 1 - 2 * half

    barrier = pltpu.get_barrier_semaphore()

    def peer_of(d):
        return lax.rem(frame + d, frames)

    def greet_ctx(d, carry):
        pl.semaphore_signal(
            barrier, inc=1, device_id={"ctx": 2 * peer_of(d) + half}, device_id_type=MESH
        )
        return carry

    def greet_head(d, carry):
        pl.semaphore_signal(
            barrier, inc=1, device_id={"head": lax.rem(group + d, groups)}, device_id_type=MESH
        )
        return carry

    pl.semaphore_signal(barrier, inc=1, device_id={"ctx": partner}, device_id_type=MESH)
    lax.fori_loop(1, frames, greet_ctx, 0)
    lax.fori_loop(1, groups, greet_head, 0)

    one_hot = {}
    seen = jnp.zeros((1, HDIM), jnp.int32)
    for h in range(heads):
        kind = jnp.full((1, HDIM), kind_ref[group * heads + h], jnp.int32)
        for slot in range(NT + NS):
            if slot < NT:
                chosen = (kind == 1) & (seen == slot)
            else:
                chosen = (kind == 0) & (h - seen == slot - NT)
            one_hot[slot, h] = jnp.where(chosen, 1.0, 0.0).astype(BF16)
        seen = seen + kind

    def fits(slot, h):
        if slot < NT:
            return h >= slot
        return 0 <= h - (slot - NT) <= NT

    def pick(ref, slot):
        total = None
        for h in range(heads):
            if fits(slot, h):
                term = ref[:, h * HDIM : (h + 1) * HDIM] * one_hot[slot, h]
                total = term if total is None else total + term
        return total

    for j in range(NT):
        vt[j] = pick(v_ref, j).reshape(frames, block, HDIM)

    pl.semaphore_wait(barrier, frames - 1 + groups - 1 + 1)

    def send_v(j):
        def step(d, carry):
            to = peer_of(d)
            pltpu.make_async_remote_copy(
                src_ref=vt.at[j, to], dst_ref=vr.at[j, frame],
                send_sem=vt_send.at[j], recv_sem=vt_recv.at[j],
                device_id={"ctx": 2 * to + half}, device_id_type=MESH,
            ).start()
            return carry
        lax.fori_loop(1, frames, step, 0)

    def send_qk(j):
        def step(d, carry):
            to = peer_of(d)
            pltpu.make_async_remote_copy(
                src_ref=qkt.at[j, :, to], dst_ref=qkr.at[j, :, frame],
                send_sem=qk_send.at[j], recv_sem=qk_recv.at[j],
                device_id={"ctx": 2 * to + half}, device_id_type=MESH,
            ).start()
            return carry
        lax.fori_loop(1, frames, step, 0)

    def send_ret(j):
        def step(d, carry):
            to = peer_of(d)
            pltpu.make_async_remote_copy(
                src_ref=ot.at[j, to], dst_ref=res.at[j, frame],
                send_sem=ret_send.at[j], recv_sem=ret_recv.at[j],
                device_id={"ctx": 2 * to + half}, device_id_type=MESH,
            ).start()
            return carry
        lax.fori_loop(1, frames, step, 0)

    def pair_copy(src, dst, send, recv, j):
        return pltpu.make_async_remote_copy(
            src_ref=src.at[j], dst_ref=dst.at[j], send_sem=send.at[j], recv_sem=recv.at[j],
            device_id={"ctx": partner}, device_id_type=MESH,
        )

    def wait_bytes(ref, sem):
        pltpu.make_async_copy(ref, ref, sem).wait()

    for j in range(NT):
        send_v(j)

    sub = lax.broadcasted_iota(jnp.int32, (8, CHUNK), 0)

    def squares(i, carry):
        rows = pl.ds(pl.multiple_of(i * CHUNK, CHUNK), CHUNK)
        kept = []
        for ref, tile in ((q_ref, carry[0]), (k_ref, carry[1])):
            part = ref[rows, :].astype(F32)
            total = jnp.sum(part * part, axis=1, keepdims=True)
            row = jnp.broadcast_to(total, (CHUNK, CHUNK)).T[0:8]
            kept.append(jnp.where(sub == i, row, tile))
        return tuple(kept)

    zero = jnp.zeros((8, CHUNK), F32)
    tiles = lax.fori_loop(0, chunks, squares, (zero, zero))
    for n in range(2):
        ss_own[n] = tiles[n]
        ss_all[group, n] = tiles[n]

    def send_squares(d, carry):
        pltpu.make_async_remote_copy(
            src_ref=ss_own, dst_ref=ss_all.at[group],
            send_sem=ss_sems.at[0], recv_sem=ss_sems.at[1],
            device_id={"head": lax.rem(group + d, groups)}, device_id_type=MESH,
        ).start()
        return carry

    lax.fori_loop(1, groups, send_squares, 0)

    for j in range(NS):
        own_v[j] = pick(v_ref, NT + j)

    wait_bytes(ss_all.at[pl.ds(0, groups - 1)], ss_sems.at[1])
    for n, column in ((0, rq), (1, rk)):
        total = ss_all[0, n]
        for g in range(1, groups):
            total = total + ss_all[g, n]
        inverse = lax.rsqrt(total * (1.0 / (HEADS * HDIM)) + EPSILON)
        for i in range(chunks):
            column[pl.ds(i * CHUNK, CHUNK), :] = jnp.broadcast_to(
                inverse[i : i + 1, :], (CHUNK, CHUNK)
            ).T

    for h in range(heads):
        at = slice(h * HDIM, (h + 1) * HDIM)
        qn[:, at] = (q_ref[:, at].astype(F32) * rq[...] * gq_ref[:, at]).astype(BF16)
        kn[:, at] = (k_ref[:, at].astype(F32) * rk[...] * gk_ref[:, at]).astype(BF16)

    for j in range(NT):
        qkt[j, 0] = pick(qn, j).reshape(frames, block, HDIM)
        qkt[j, 1] = pick(kn, j).reshape(frames, block, HDIM)
        send_qk(j)
        vr[j, frame] = vt[j, frame]
        for n in range(2):
            qkr[j, n, frame] = qkt[j, n, frame]

    for j in range(NS):
        own_k[j] = pick(kn, NT + j)
        pair_copy(own_k, par_k, sk_send, sk_recv, j).start()
        pair_copy(own_v, par_v, sv_send, sv_recv, j).start()
        qs[j] = pick(qn, NT + j)

    step_rows = 16 * frames
    same = (
        lax.rem(lax.broadcasted_iota(jnp.int32, (step_rows, step_rows), 0), 16)
        == lax.rem(lax.broadcasted_iota(jnp.int32, (step_rows, step_rows), 1), 16)
    )
    for j in range(NT):
        wait_bytes(vr.at[j, pl.ds(0, frames - 1)], vt_recv.at[j])
        wait_bytes(qkr.at[j, :, pl.ds(0, frames - 1)], qk_recv.at[j])
        for c in range(block // 16):
            at = pl.ds(c * 16, 16)
            query = qkr[j, 0, :, at, :].reshape(step_rows, HDIM)
            key = qkr[j, 1, :, at, :].reshape(step_rows, HDIM)
            value = vr[j, :, at, :].reshape(step_rows, HDIM)
            scores = jnp.where(same, dot_nt(query, key) * score_scale, -jnp.inf)
            expo = jnp.exp(scores - jnp.max(scores, axis=1, keepdims=True))
            weights = (expo / jnp.sum(expo, axis=1, keepdims=True)).astype(BF16)
            mixed = dot_nn(weights, value).astype(BF16)
            ot[j, :, at, :] = mixed.reshape(frames, 16, HDIM)
        send_ret(j)
        res[j, frame] = ot[j, frame]

    def spatial(j, carry):
        pair_copy(own_k, par_k, sk_send, sk_recv, j).wait_recv()
        pair_copy(own_v, par_v, sv_send, sv_recv, j).wait_recv()
        own_key, own_value, par_key, par_value = own_k[j], own_v[j], par_k[j], par_v[j]

        def rows_step(i, inner):
            query = qs[j, pl.ds(pl.multiple_of(i * QROWS, QROWS), QROWS), :]
            s_own = dot_nt(query, own_key) * score_scale
            s_par = dot_nt(query, par_key) * score_scale
            top = jnp.maximum(
                jnp.max(s_own, axis=1, keepdims=True), jnp.max(s_par, axis=1, keepdims=True)
            )
            e_own = jnp.exp(s_own - top)
            e_par = jnp.exp(s_par - top)
            total = jnp.sum(e_own, axis=1, keepdims=True) + jnp.sum(e_par, axis=1, keepdims=True)
            mixed = dot_nn(e_own.astype(BF16), own_value) + dot_nn(e_par.astype(BF16), par_value)
            per = QROWS // block
            res[NT + j, pl.ds(i * per, per)] = (
                (mixed / total).astype(BF16).reshape(per, block, HDIM)
            )
            return inner

        return lax.fori_loop(0, tokens // QROWS, rows_step, carry)

    lax.fori_loop(0, NS, spatial, 0)

    for j in range(NT):
        wait_bytes(res.at[j, pl.ds(0, frames - 1)], ret_recv.at[j])
    for h in range(heads):
        total = None
        for slot in range(NT + NS):
            if fits(slot, h):
                term = res[slot].reshape(tokens, HDIM) * one_hot[slot, h]
                total = term if total is None else total + term
        out_ref[:, h * HDIM : (h + 1) * HDIM] = total

    wait_bytes(ss_all.at[pl.ds(0, groups - 1)], ss_sems.at[0])
    for j in range(NT):
        wait_bytes(vt.at[j, pl.ds(0, frames - 1)], vt_send.at[j])
        wait_bytes(qkt.at[j, :, pl.ds(0, frames - 1)], qk_send.at[j])
        wait_bytes(ot.at[j, pl.ds(0, frames - 1)], ret_send.at[j])
    for j in range(NS):
        pair_copy(own_k, par_k, sk_send, sk_recv, j).wait_send()
        pair_copy(own_v, par_v, sv_send, sv_recv, j).wait_send()


def shards(query, key, value, gain_q, gain_k, head_kind):
    tokens, width = query.shape
    frames = lax.axis_size("ctx") // 2
    groups = lax.axis_size("head")
    block = tokens // frames
    vmem = pl.BlockSpec(memory_space=pltpu.VMEM)
    dma = pltpu.SemaphoreType.DMA
    return pl.pallas_call(
        functools.partial(kernel, frames, groups),
        out_shape=jax.ShapeDtypeStruct((tokens, width), BF16),
        in_specs=[pl.BlockSpec(memory_space=pltpu.SMEM)] + [vmem] * 5,
        out_specs=vmem,
        scratch_shapes=[
            pltpu.VMEM((NT, frames, block, HDIM), BF16),
            pltpu.VMEM((NT, 2, frames, block, HDIM), BF16),
            pltpu.VMEM((NT, frames, block, HDIM), BF16),
            pltpu.VMEM((NT, 2, frames, block, HDIM), BF16),
            pltpu.VMEM((NT, frames, block, HDIM), BF16),
            pltpu.VMEM((NT + NS, frames, block, HDIM), BF16),
            pltpu.VMEM((NS, tokens, HDIM), BF16),
            pltpu.VMEM((NS, tokens, HDIM), BF16),
            pltpu.VMEM((NS, tokens, HDIM), BF16),
            pltpu.VMEM((NS, tokens, HDIM), BF16),
            pltpu.VMEM((NS, tokens, HDIM), BF16),
            pltpu.VMEM((tokens, width), BF16),
            pltpu.VMEM((tokens, width), BF16),
            pltpu.VMEM((tokens, HDIM), F32),
            pltpu.VMEM((tokens, HDIM), F32),
            pltpu.VMEM((2, 8, CHUNK), F32),
            pltpu.VMEM((groups, 2, 8, CHUNK), F32),
            dma((2,)),
            dma((NT,)), dma((NT,)), dma((NT,)), dma((NT,)), dma((NT,)), dma((NT,)),
            dma((NS,)), dma((NS,)), dma((NS,)), dma((NS,)),
        ],
        compiler_params=pltpu.CompilerParams(
            collective_id=0, has_side_effects=True, vmem_limit_bytes=56 * 2**20
        ),
        cost_estimate=pl.CostEstimate(
            flops=4 * NS * tokens * 2 * tokens * HDIM,
            bytes_accessed=8 * tokens * width,
            transcendentals=NS * 2 * tokens * tokens,
        ),
        name="head_attention",
    )(head_kind, query, key, value, gain_q.reshape(1, -1), gain_k.reshape(1, -1))


def solution(mesh):
    return jax.shard_map(
        shards,
        mesh=mesh,
        in_specs=(P("ctx", "head"), P("ctx", "head"), P("ctx", "head"), P("head"), P("head"), P()),
        out_specs=P("ctx", "head"),
        check_vma=False,
    )
```

```python
import functools
import math

import jax
import jax.numpy as jnp
from jax import lax
from jax.experimental import pallas as pl
from jax.experimental.pallas import tpu as pltpu
from jax.sharding import PartitionSpec as P

HEADS = 40
HDIM = 128
EPSILON = 1e-06
NT = 3
NS = 4
ND = 2
FLEX = (2, 1)
SPATIAL_OF = {2: 2, 1: 3}
MZ = 4
PAD = 256
CHUNK = 128
QROWS = 256
MESH = pl.DeviceIdType.MESH
BF16 = jnp.bfloat16
F32 = jnp.float32


def dot_nt(a, b):
    return lax.dot_general(a, b, (((1,), (1,)), ((), ())), preferred_element_type=F32)


def dot_nn(a, b):
    return lax.dot_general(a, b, (((1,), (0,)), ((), ())), preferred_element_type=F32)


def kernel(
    frames, groups, kind_ref, q_ref, k_ref, v_ref, gq_ref, gk_ref, out_ref,
    snd, rcv, ot, res, own, par, qs, qn, kn, rq, rk, ss_own, ss_all, out_msg, near_msg, far_msg,
    ss_sems, va_sems, qka_sems, ret_send, ret_recv, k_sems, v_sems,
    near_sems, out_send, out_recv, far_sems, fwd_send, fwd_recv,
):
    tokens, width = q_ref.shape
    heads = width // HDIM
    block = tokens // frames
    chunks = tokens // CHUNK
    score_scale = 1.0 / math.sqrt(HDIM)
    ctx = lax.axis_index("ctx")
    group = lax.axis_index("head")
    frame, half = ctx // 2, ctx % 2
    y, m = frame // MZ, frame % MZ
    sign = 1 - 2 * half
    partner = ctx + 1 - 2 * half
    ny = frames // MZ

    def frame_at(dy, dm):
        return lax.rem(y + dy + ny, ny) * MZ + lax.rem(m + dm + MZ, MZ)

    def to_ctx(to_frame, to_half):
        return {"ctx": 2 * to_frame + to_half}

    in_frames = [frame_at(b, sign) for b in range(4)] + [frame_at(b, 2) for b in (0, 1)]
    out_frames = [frame_at(b, -sign) for b in range(4)] + [frame_at(b, 2) for b in (2, 3)]

    barrier = pltpu.get_barrier_semaphore()

    def greet(device_id):
        pl.semaphore_signal(barrier, inc=1, device_id=device_id, device_id_type=MESH)

    def peer_of(d):
        return lax.rem(frame + d, frames)

    def greet_ctx(d, carry):
        greet(to_ctx(peer_of(d), half))
        return carry

    def greet_head(d, carry):
        greet({"head": lax.rem(group + d, groups)})
        return carry

    greet({"ctx": partner})
    for b in range(4):
        greet(to_ctx(frame_at(b, -sign), 1 - half))
    for b in (0, 1, 3):
        greet(to_ctx(frame_at(b, 2), 1 - half))
    lax.fori_loop(1, frames, greet_ctx, 0)
    lax.fori_loop(1, groups, greet_head, 0)

    one_hot = {}
    seen = jnp.zeros((1, HDIM), jnp.int32)
    for h in range(heads):
        kind = jnp.full((1, HDIM), kind_ref[group * heads + h], jnp.int32)
        for slot in range(NT + NS):
            if slot < NT:
                chosen = (kind == 1) & (seen == slot)
            else:
                chosen = (kind == 0) & (h - seen == slot - NT)
            one_hot[slot, h] = jnp.where(chosen, 1.0, 0.0).astype(BF16)
        seen = seen + kind

    def fits(slot, h):
        if slot < NT:
            return h >= slot
        return 0 <= h - (slot - NT) <= NT

    def pick(ref, slot):
        total = None
        for h in range(heads):
            if fits(slot, h):
                term = ref[:, h * HDIM : (h + 1) * HDIM] * one_hot[slot, h]
                total = term if total is None else total + term
        return total

    V, Q, K = (pl.ds(n * block, block) for n in range(3))
    KEYS, VALUES = pl.ds(0, tokens), pl.ds(tokens, tokens)

    def blocks_of(x):
        return x.reshape(frames, block, HDIM)

    def remote(src, dst, send, recv, device_id):
        return pltpu.make_async_remote_copy(
            src_ref=src, dst_ref=dst, send_sem=send, recv_sem=recv,
            device_id=device_id, device_id_type=MESH,
        )

    def wait_bytes(ref, sem):
        pltpu.make_async_copy(ref, ref, sem).wait()

    def pair_keys(j):
        return remote(own.at[j, KEYS], par.at[j, KEYS], k_sems.at[0, j], k_sems.at[1, j], {"ctx": partner})

    def pair_values(j):
        return remote(own.at[j, VALUES], par.at[j, VALUES], v_sems.at[0, j], v_sems.at[1, j], {"ctx": partner})

    snd[0, :, V, :] = blocks_of(pick(v_ref, 0))

    pl.semaphore_wait(barrier, frames - 1 + groups - 1 + 8)

    def send_va(d, carry):
        to = peer_of(d)
        remote(
            snd.at[0, to, V], rcv.at[0, frame, V], va_sems.at[0], va_sems.at[1], to_ctx(to, half)
        ).start()
        return carry

    lax.fori_loop(1, frames, send_va, 0)
    for j in range(ND):
        own[j, VALUES, :] = pick(v_ref, NT + j)
        pair_values(j).start()

    sub = lax.broadcasted_iota(jnp.int32, (8, CHUNK), 0)

    def squares(i, carry):
        rows = pl.ds(pl.multiple_of(i * CHUNK, CHUNK), CHUNK)
        kept = []
        for ref, tile in ((q_ref, carry[0]), (k_ref, carry[1])):
            part = ref[rows, :].astype(F32)
            total = jnp.sum(part * part, axis=1, keepdims=True)
            row = jnp.broadcast_to(total, (CHUNK, CHUNK)).T[0:8]
            kept.append(jnp.where(sub == i, row, tile))
        return tuple(kept)

    zero = jnp.zeros((8, CHUNK), F32)
    tiles = lax.fori_loop(0, chunks, squares, (zero, zero))
    for n in range(2):
        ss_own[n] = tiles[n]
        ss_all[group, n] = tiles[n]

    def send_squares(d, carry):
        remote(
            ss_own, ss_all.at[group], ss_sems.at[0], ss_sems.at[1],
            {"head": lax.rem(group + d, groups)},
        ).start()
        return carry

    lax.fori_loop(1, groups, send_squares, 0)

    for j in FLEX:
        snd[j, :, V, :] = blocks_of(pick(v_ref, j))
        own[SPATIAL_OF[j], VALUES, :] = pick(v_ref, NT + SPATIAL_OF[j])
        own[SPATIAL_OF[j], pl.ds(2 * tokens, PAD), :] = jnp.zeros((PAD, HDIM), BF16)

    wait_bytes(ss_all.at[pl.ds(0, groups - 1)], ss_sems.at[1])
    for n, column in ((0, rq), (1, rk)):
        total = ss_all[0, n]
        for g in range(1, groups):
            total = total + ss_all[g, n]
        inverse = lax.rsqrt(total * (1.0 / (HEADS * HDIM)) + EPSILON)
        for i in range(chunks):
            column[pl.ds(i * CHUNK, CHUNK), :] = jnp.broadcast_to(
                inverse[i : i + 1, :], (CHUNK, CHUNK)
            ).T

    for h in range(heads):
        at = slice(h * HDIM, (h + 1) * HDIM)
        qn[:, at] = (q_ref[:, at].astype(F32) * rq[...] * gq_ref[:, at]).astype(BF16)
        kn[:, at] = (k_ref[:, at].astype(F32) * rk[...] * gk_ref[:, at]).astype(BF16)

    size = 3 * block

    def near_copy(j):
        s = SPATIAL_OF[j]
        return remote(
            near_msg.at[j - 1], par.at[s, pl.ds(0, 6 * size)],
            near_sems.at[0, j - 1], near_sems.at[1, j - 1], {"ctx": partner},
        )

    def far_copy(j):
        s = SPATIAL_OF[j]
        return remote(
            far_msg.at[j - 1], par.at[s, pl.ds(6 * size, 6 * size)],
            far_sems.at[0, j - 1], far_sems.at[1, j - 1], {"ctx": partner},
        )

    for j in FLEX:
        s = SPATIAL_OF[j]
        snd[j, :, Q, :] = blocks_of(pick(qn, j))
        snd[j, :, K, :] = blocks_of(pick(kn, j))
        for b in range(6):
            remote(
                snd.at[j, out_frames[b]], out_msg.at[j - 1, pl.ds(b * size, size)],
                out_send.at[j - 1], out_recv.at[j - 1], to_ctx(frame_at(0, -sign), 1 - half),
            ).start()
        own[s, KEYS, :] = pick(kn, NT + s)
        for b in range(6):
            near_msg[j - 1, pl.ds(b * size, size), :] = (
                snd[j, in_frames[b]] + own[s, pl.ds(b * size, size), :]
            )
        near_copy(j).start()
        for b in range(1, 4):
            remote(
                snd.at[j, frame_at(b, 0)], rcv.at[j, frame],
                fwd_send.at[j - 1], fwd_recv.at[j - 1], to_ctx(frame_at(b, 0), half),
            ).start()
        rcv[j, frame] = snd[j, frame]
        qs[s] = pick(qn, NT + s)

    snd[0, :, Q, :] = blocks_of(pick(qn, 0))
    snd[0, :, K, :] = blocks_of(pick(kn, 0))
    QK = pl.ds(block, 2 * block)

    def send_qka(d, carry):
        to = peer_of(d)
        remote(
            snd.at[0, to, QK], rcv.at[0, frame, QK], qka_sems.at[0], qka_sems.at[1], to_ctx(to, half)
        ).start()
        return carry

    lax.fori_loop(1, frames, send_qka, 0)
    rcv[0, frame] = snd[0, frame]

    for j in FLEX:
        s = SPATIAL_OF[j]
        wait_bytes(out_msg.at[j - 1], out_recv.at[j - 1])
        for b in range(6):
            at = pl.ds(b * size, size)
            far_msg[j - 1, at, :] = out_msg[j - 1, at, :] + own[s, pl.ds((6 + b) * size, size), :]
        far_copy(j).start()

    for j in range(ND):
        own[j, KEYS, :] = pick(kn, NT + j)
        pair_keys(j).start()
        qs[j] = pick(qn, NT + j)

    for j in FLEX:
        s = SPATIAL_OF[j]
        near_copy(j).wait_recv()
        for b in range(6):
            to = frame_at(b, -sign) if b < 4 else frame_at(b - 4, 2)
            remote(
                par.at[s, pl.ds(b * size, size)], rcv.at[j, frame],
                fwd_send.at[j - 1], fwd_recv.at[j - 1], to_ctx(to, 1 - half),
            ).start()
    for j in FLEX:
        s = SPATIAL_OF[j]
        far_copy(j).wait_recv()
        origin = frame_at(0, sign)
        for b in range(1, 6):
            to = frame_at(b, 0) if b < 4 else frame_at(b - 2, -sign)
            remote(
                par.at[s, pl.ds((6 + b) * size, size)], rcv.at[j, origin],
                fwd_send.at[j - 1], fwd_recv.at[j - 1], to_ctx(to, half),
            ).start()
        rcv[j, origin] = par[s, pl.ds(6 * size, size), :]

    step_rows = 16 * frames
    same = (
        lax.rem(lax.broadcasted_iota(jnp.int32, (step_rows, step_rows), 0), 16)
        == lax.rem(lax.broadcasted_iota(jnp.int32, (step_rows, step_rows), 1), 16)
    )

    def temporal(j):
        def rows(n, c):
            return rcv[j, :, pl.ds(n * block + c * 16, 16), :].reshape(step_rows, HDIM)

        for c in range(block // 16):
            value, query, key = rows(0, c), rows(1, c), rows(2, c)
            scores = jnp.where(same, dot_nt(query, key) * score_scale, -jnp.inf)
            expo = jnp.exp(scores - jnp.max(scores, axis=1, keepdims=True))
            weights = (expo / jnp.sum(expo, axis=1, keepdims=True)).astype(BF16)
            mixed = dot_nn(weights, value).astype(BF16)
            ot[j, :, pl.ds(c * 16, 16), :] = mixed.reshape(frames, 16, HDIM)

        def send_ret(d, carry):
            to = peer_of(d)
            remote(
                ot.at[j, to], res.at[j, frame], ret_send.at[j], ret_recv.at[j], to_ctx(to, half)
            ).start()
            return carry

        lax.fori_loop(1, frames, send_ret, 0)
        res[j, frame] = ot[j, frame]

    def spatial(j):
        own_key, own_value, par_key, par_value = own[j, KEYS], own[j, VALUES], par[j, KEYS], par[j, VALUES]

        def rows_step(i, inner):
            query = qs[j, pl.ds(pl.multiple_of(i * QROWS, QROWS), QROWS), :]
            s_own = dot_nt(query, own_key) * score_scale
            s_par = dot_nt(query, par_key) * score_scale
            top = jnp.maximum(
                jnp.max(s_own, axis=1, keepdims=True), jnp.max(s_par, axis=1, keepdims=True)
            )
            e_own = jnp.exp(s_own - top)
            e_par = jnp.exp(s_par - top)
            total = jnp.sum(e_own, axis=1, keepdims=True) + jnp.sum(e_par, axis=1, keepdims=True)
            mixed = dot_nn(e_own.astype(BF16), own_value) + dot_nn(e_par.astype(BF16), par_value)
            per = QROWS // block
            res[NT + j, pl.ds(i * per, per)] = (
                (mixed / total).astype(BF16).reshape(per, block, HDIM)
            )
            return inner

        lax.fori_loop(0, tokens // QROWS, rows_step, 0)

    wait_bytes(rcv.at[0, pl.ds(0, frames - 1), V], va_sems.at[1])
    wait_bytes(rcv.at[0, pl.ds(0, frames - 1), QK], qka_sems.at[1])
    temporal(0)
    for j in FLEX:
        wait_bytes(rcv.at[j, pl.ds(0, frames - 2)], fwd_recv.at[j - 1])
        temporal(j)

    for j in range(ND):
        pair_values(j).wait_recv()
        pair_keys(j).wait_recv()

    def spatial_step(j, carry):
        spatial(j)
        return carry

    lax.fori_loop(0, NS, spatial_step, 0)

    for j in range(NT):
        wait_bytes(res.at[j, pl.ds(0, frames - 1)], ret_recv.at[j])
    for h in range(heads):
        total = None
        for slot in range(NT + NS):
            if fits(slot, h):
                term = res[slot].reshape(tokens, HDIM) * one_hot[slot, h]
                total = term if total is None else total + term
        out_ref[:, h * HDIM : (h + 1) * HDIM] = total

    wait_bytes(ss_all.at[pl.ds(0, groups - 1)], ss_sems.at[0])
    wait_bytes(snd.at[0, pl.ds(0, frames - 1), V], va_sems.at[0])
    wait_bytes(snd.at[0, pl.ds(0, frames - 1), QK], qka_sems.at[0])
    for j in range(NT):
        wait_bytes(ot.at[j, pl.ds(0, frames - 1)], ret_send.at[j])
    for j in FLEX:
        wait_bytes(out_msg.at[j - 1], out_send.at[j - 1])
        near_copy(j).wait_send()
        far_copy(j).wait_send()
        wait_bytes(rcv.at[j, pl.ds(0, frames - 2)], fwd_send.at[j - 1])
    for j in range(ND):
        pair_keys(j).wait_send()
        pair_values(j).wait_send()


def shards(query, key, value, gain_q, gain_k, head_kind):
    tokens, width = query.shape
    frames = lax.axis_size("ctx") // 2
    groups = lax.axis_size("head")
    block = tokens // frames
    vmem = pl.BlockSpec(memory_space=pltpu.VMEM)
    dma = pltpu.SemaphoreType.DMA
    return pl.pallas_call(
        functools.partial(kernel, frames, groups),
        out_shape=jax.ShapeDtypeStruct((tokens, width), BF16),
        in_specs=[pl.BlockSpec(memory_space=pltpu.SMEM)] + [vmem] * 5,
        out_specs=vmem,
        scratch_shapes=[
            pltpu.VMEM((NT, frames, 3 * block, HDIM), BF16),
            pltpu.VMEM((NT, frames, 3 * block, HDIM), BF16),
            pltpu.VMEM((NT, frames, block, HDIM), BF16),
            pltpu.VMEM((NT + NS, frames, block, HDIM), BF16),
            pltpu.VMEM((NS, 2 * tokens + PAD, HDIM), BF16),
            pltpu.VMEM((NS, 2 * tokens + PAD, HDIM), BF16),
            pltpu.VMEM((NS, tokens, HDIM), BF16),
            pltpu.VMEM((tokens, width), BF16),
            pltpu.VMEM((tokens, width), BF16),
            pltpu.VMEM((tokens, HDIM), F32),
            pltpu.VMEM((tokens, HDIM), F32),
            pltpu.VMEM((2, 8, CHUNK), F32),
            pltpu.VMEM((groups, 2, 8, CHUNK), F32),
            pltpu.VMEM((2, 18 * block, HDIM), BF16),
            pltpu.VMEM((2, 18 * block, HDIM), BF16),
            pltpu.VMEM((2, 18 * block, HDIM), BF16),
            dma((2,)), dma((2,)), dma((2,)), dma((NT,)), dma((NT,)), dma((2, ND)), dma((2, ND)),
            dma((2, 2)), dma((2,)), dma((2,)), dma((2, 2)), dma((2,)), dma((2,)),
        ],
        compiler_params=pltpu.CompilerParams(
            collective_id=0, has_side_effects=True, vmem_limit_bytes=56 * 2**20
        ),
        cost_estimate=pl.CostEstimate(
            flops=4 * NS * tokens * 2 * tokens * HDIM,
            bytes_accessed=8 * tokens * width,
            transcendentals=NS * 2 * tokens * tokens,
        ),
        name="head_attention",
    )(head_kind, query, key, value, gain_q.reshape(1, -1), gain_k.reshape(1, -1))


def solution(mesh):
    return jax.shard_map(
        shards,
        mesh=mesh,
        in_specs=(P("ctx", "head"), P("ctx", "head"), P("ctx", "head"), P("head"), P("head"), P()),
        out_specs=P("ctx", "head"),
        check_vma=False,
    )
```

```python
import functools
import math

import jax
import jax.numpy as jnp
from jax import lax
from jax.experimental import pallas as pl
from jax.experimental.pallas import tpu as pltpu
from jax.sharding import PartitionSpec as P

HEADS = 40
HDIM = 128
EPSILON = 1e-06
NT = 3
NS = 4
ND = 2
FLEX = (2, 1)
SPATIAL_OF = {2: 2, 1: 3}
MZ = 4
PAD = 256
CHUNK = 128
QROWS = 256
MESH = pl.DeviceIdType.MESH
BF16 = jnp.bfloat16
F32 = jnp.float32


def dot_nt(a, b):
    return lax.dot_general(a, b, (((1,), (1,)), ((), ())), preferred_element_type=F32)


def dot_nn(a, b):
    return lax.dot_general(a, b, (((1,), (0,)), ((), ())), preferred_element_type=F32)


def kernel(
    frames, groups, kind_ref, q_ref, k_ref, v_ref, gq_ref, gk_ref, out_ref,
    snd, rcv, ot, res, own, par, qs, qn, kn, rq, rk, ss_own, ss_all, out_msg, near_msg, far_msg,
    ss_sems, va_sems, qka_sems, ret_send, ret_recv, k_sems, v_sems,
    near_sems, out_send, out_recv, far_sems, fwd_send, fwd_recv,
):
    tokens, width = q_ref.shape
    heads = width // HDIM
    block = tokens // frames
    chunks = tokens // CHUNK
    score_scale = 1.0 / math.sqrt(HDIM)
    ctx = lax.axis_index("ctx")
    group = lax.axis_index("head")
    frame, half = ctx // 2, ctx % 2
    y, m = frame // MZ, frame % MZ
    sign = 1 - 2 * half
    partner = ctx + 1 - 2 * half
    ny = frames // MZ

    def frame_at(dy, dm):
        return lax.rem(y + dy + ny, ny) * MZ + lax.rem(m + dm + MZ, MZ)

    def to_ctx(to_frame, to_half):
        return {"ctx": 2 * to_frame + to_half}

    in_frames = [frame_at(b, sign) for b in range(4)] + [frame_at(b, 2) for b in (0, 1)]
    out_frames = [frame_at(b, -sign) for b in range(4)] + [frame_at(b, 2) for b in (2, 3)]

    barrier = pltpu.get_barrier_semaphore()

    def greet(device_id):
        pl.semaphore_signal(barrier, inc=1, device_id=device_id, device_id_type=MESH)

    def peer_of(d):
        return lax.rem(frame + d, frames)

    def greet_ctx(d, carry):
        greet(to_ctx(peer_of(d), half))
        return carry

    def greet_head(d, carry):
        greet({"head": lax.rem(group + d, groups)})
        return carry

    greet({"ctx": partner})
    for b in range(4):
        greet(to_ctx(frame_at(b, -sign), 1 - half))
    for b in (0, 1, 3):
        greet(to_ctx(frame_at(b, 2), 1 - half))
    lax.fori_loop(1, frames, greet_ctx, 0)
    lax.fori_loop(1, groups, greet_head, 0)

    one_hot = {}
    seen = jnp.zeros((1, HDIM), jnp.int32)
    for h in range(heads):
        kind = jnp.full((1, HDIM), kind_ref[group * heads + h], jnp.int32)
        for slot in range(NT + NS):
            if slot < NT:
                chosen = (kind == 1) & (seen == slot)
            else:
                chosen = (kind == 0) & (h - seen == slot - NT)
            one_hot[slot, h] = jnp.where(chosen, 1.0, 0.0).astype(BF16)
        seen = seen + kind

    def fits(slot, h):
        if slot < NT:
            return h >= slot
        return 0 <= h - (slot - NT) <= NT

    def pick(ref, slot):
        total = None
        for h in range(heads):
            if fits(slot, h):
                term = ref[:, h * HDIM : (h + 1) * HDIM] * one_hot[slot, h]
                total = term if total is None else total + term
        return total

    V, Q, K = (pl.ds(n * block, block) for n in range(3))
    KEYS, VALUES = pl.ds(0, tokens), pl.ds(tokens, tokens)

    def blocks_of(x):
        return x.reshape(frames, block, HDIM)

    def remote(src, dst, send, recv, device_id):
        return pltpu.make_async_remote_copy(
            src_ref=src, dst_ref=dst, send_sem=send, recv_sem=recv,
            device_id=device_id, device_id_type=MESH,
        )

    def wait_bytes(ref, sem):
        pltpu.make_async_copy(ref, ref, sem).wait()

    def pair_keys(j):
        return remote(own.at[j, KEYS], par.at[j, KEYS], k_sems.at[0, j], k_sems.at[1, j], {"ctx": partner})

    def pair_values(j):
        return remote(own.at[j, VALUES], par.at[j, VALUES], v_sems.at[0, j], v_sems.at[1, j], {"ctx": partner})

    snd[0, :, V, :] = blocks_of(pick(v_ref, 0))

    pl.semaphore_wait(barrier, frames - 1 + groups - 1 + 8)

    def send_va(d, carry):
        to = peer_of(d)
        remote(
            snd.at[0, to, V], rcv.at[0, frame, V], va_sems.at[0], va_sems.at[1], to_ctx(to, half)
        ).start()
        return carry

    lax.fori_loop(1, frames, send_va, 0)
    for j in (0,):
        own[j, VALUES, :] = pick(v_ref, NT + j)
        pair_values(j).start()

    sub = lax.broadcasted_iota(jnp.int32, (8, CHUNK), 0)

    def squares(i, carry):
        rows = pl.ds(pl.multiple_of(i * CHUNK, CHUNK), CHUNK)
        kept = []
        for ref, tile in ((q_ref, carry[0]), (k_ref, carry[1])):
            part = ref[rows, :].astype(F32)
            total = jnp.sum(part * part, axis=1, keepdims=True)
            row = jnp.broadcast_to(total, (CHUNK, CHUNK)).T[0:8]
            kept.append(jnp.where(sub == i, row, tile))
        return tuple(kept)

    zero = jnp.zeros((8, CHUNK), F32)
    tiles = lax.fori_loop(0, chunks, squares, (zero, zero))
    for n in range(2):
        ss_own[n] = tiles[n]
        ss_all[group, n] = tiles[n]

    def send_squares(d, carry):
        remote(
            ss_own, ss_all.at[group], ss_sems.at[0], ss_sems.at[1],
            {"head": lax.rem(group + d, groups)},
        ).start()
        return carry

    lax.fori_loop(1, groups, send_squares, 0)

    for j in FLEX:
        snd[j, :, V, :] = blocks_of(pick(v_ref, j))
        own[SPATIAL_OF[j], VALUES, :] = pick(v_ref, NT + SPATIAL_OF[j])
        own[SPATIAL_OF[j], pl.ds(2 * tokens, PAD), :] = jnp.zeros((PAD, HDIM), BF16)

    wait_bytes(ss_all.at[pl.ds(0, groups - 1)], ss_sems.at[1])
    for n, column in ((0, rq), (1, rk)):
        total = ss_all[0, n]
        for g in range(1, groups):
            total = total + ss_all[g, n]
        inverse = lax.rsqrt(total * (1.0 / (HEADS * HDIM)) + EPSILON)
        for i in range(chunks):
            column[pl.ds(i * CHUNK, CHUNK), :] = jnp.broadcast_to(
                inverse[i : i + 1, :], (CHUNK, CHUNK)
            ).T

    for h in range(heads):
        at = slice(h * HDIM, (h + 1) * HDIM)
        qn[:, at] = (q_ref[:, at].astype(F32) * rq[...] * gq_ref[at]).astype(BF16)
        kn[:, at] = (k_ref[:, at].astype(F32) * rk[...] * gk_ref[at]).astype(BF16)

    size = 3 * block

    def near_copy(j):
        s = SPATIAL_OF[j]
        return remote(
            near_msg.at[j - 1], par.at[s, pl.ds(0, 6 * size)],
            near_sems.at[0, j - 1], near_sems.at[1, j - 1], {"ctx": partner},
        )

    def far_copy(j):
        s = SPATIAL_OF[j]
        return remote(
            far_msg.at[j - 1], par.at[s, pl.ds(6 * size, 6 * size)],
            far_sems.at[0, j - 1], far_sems.at[1, j - 1], {"ctx": partner},
        )

    for j in FLEX:
        s = SPATIAL_OF[j]
        snd[j, :, Q, :] = blocks_of(pick(qn, j))
        snd[j, :, K, :] = blocks_of(pick(kn, j))
        for b in range(6):
            remote(
                snd.at[j, out_frames[b]], out_msg.at[j - 1, pl.ds(b * size, size)],
                out_send.at[j - 1], out_recv.at[j - 1], to_ctx(frame_at(0, -sign), 1 - half),
            ).start()
        own[s, KEYS, :] = pick(kn, NT + s)
        for b in range(6):
            near_msg[j - 1, pl.ds(b * size, size), :] = (
                snd[j, in_frames[b]] + own[s, pl.ds(b * size, size), :]
            )
        near_copy(j).start()
        for b in range(1, 4):
            remote(
                snd.at[j, frame_at(b, 0)], rcv.at[j, frame],
                fwd_send.at[j - 1], fwd_recv.at[j - 1], to_ctx(frame_at(b, 0), half),
            ).start()
        rcv[j, frame] = snd[j, frame]
        qs[s] = pick(qn, NT + s)

    for j in (0,):
        own[j, KEYS, :] = pick(kn, NT + j)
        pair_keys(j).start()
        qs[j] = pick(qn, NT + j)

    for j in FLEX:
        s = SPATIAL_OF[j]
        wait_bytes(out_msg.at[j - 1], out_recv.at[j - 1])
        for b in range(6):
            at = pl.ds(b * size, size)
            far_msg[j - 1, at, :] = out_msg[j - 1, at, :] + own[s, pl.ds((6 + b) * size, size), :]
        far_copy(j).start()

    for j in FLEX:
        s = SPATIAL_OF[j]
        near_copy(j).wait_recv()
        for b in range(6):
            to = frame_at(b, -sign) if b < 4 else frame_at(b - 4, 2)
            remote(
                par.at[s, pl.ds(b * size, size)], rcv.at[j, frame],
                fwd_send.at[j - 1], fwd_recv.at[j - 1], to_ctx(to, 1 - half),
            ).start()
    for j in (1,):
        own[j, VALUES, :] = pick(v_ref, NT + j)
        pair_values(j).start()
    for j in FLEX:
        s = SPATIAL_OF[j]
        far_copy(j).wait_recv()
        origin = frame_at(0, sign)
        for b in range(1, 6):
            to = frame_at(b, 0) if b < 4 else frame_at(b - 2, -sign)
            remote(
                par.at[s, pl.ds((6 + b) * size, size)], rcv.at[j, origin],
                fwd_send.at[j - 1], fwd_recv.at[j - 1], to_ctx(to, half),
            ).start()
        rcv[j, origin] = par[s, pl.ds(6 * size, size), :]

    snd[0, :, Q, :] = blocks_of(pick(qn, 0))
    snd[0, :, K, :] = blocks_of(pick(kn, 0))
    QK = pl.ds(block, 2 * block)

    def send_qka(d, carry):
        to = peer_of(d)
        remote(
            snd.at[0, to, QK], rcv.at[0, frame, QK], qka_sems.at[0], qka_sems.at[1], to_ctx(to, half)
        ).start()
        return carry

    lax.fori_loop(1, frames, send_qka, 0)
    rcv[0, frame] = snd[0, frame]

    for j in (1,):
        own[j, KEYS, :] = pick(kn, NT + j)
        pair_keys(j).start()
        qs[j] = pick(qn, NT + j)

    step_rows = 16 * frames
    same = (
        lax.rem(lax.broadcasted_iota(jnp.int32, (step_rows, step_rows), 0), 16)
        == lax.rem(lax.broadcasted_iota(jnp.int32, (step_rows, step_rows), 1), 16)
    )

    def temporal(j):
        def rows(n, c):
            return rcv[j, :, pl.ds(n * block + c * 16, 16), :].reshape(step_rows, HDIM)

        for c in range(block // 16):
            value, query, key = rows(0, c), rows(1, c), rows(2, c)
            scores = jnp.where(same, dot_nt(query, key) * score_scale, -jnp.inf)
            expo = jnp.exp(scores - jnp.max(scores, axis=1, keepdims=True))
            weights = (expo / jnp.sum(expo, axis=1, keepdims=True)).astype(BF16)
            mixed = dot_nn(weights, value).astype(BF16)
            ot[j, :, pl.ds(c * 16, 16), :] = mixed.reshape(frames, 16, HDIM)

        def send_ret(d, carry):
            to = peer_of(d)
            remote(
                ot.at[j, to], res.at[j, frame], ret_send.at[j], ret_recv.at[j], to_ctx(to, half)
            ).start()
            return carry

        lax.fori_loop(1, frames, send_ret, 0)
        res[j, frame] = ot[j, frame]

    def spatial(j):
        own_key, own_value, par_key, par_value = own[j, KEYS], own[j, VALUES], par[j, KEYS], par[j, VALUES]

        def rows_step(i, inner):
            query = qs[j, pl.ds(pl.multiple_of(i * QROWS, QROWS), QROWS), :]
            s_own = dot_nt(query, own_key) * score_scale
            s_par = dot_nt(query, par_key) * score_scale
            top = jnp.maximum(
                jnp.max(s_own, axis=1, keepdims=True), jnp.max(s_par, axis=1, keepdims=True)
            )
            e_own = jnp.exp(s_own - top)
            e_par = jnp.exp(s_par - top)
            total = jnp.sum(e_own, axis=1, keepdims=True) + jnp.sum(e_par, axis=1, keepdims=True)
            mixed = dot_nn(e_own.astype(BF16), own_value) + dot_nn(e_par.astype(BF16), par_value)
            per = QROWS // block
            res[NT + j, pl.ds(i * per, per)] = (
                (mixed / total).astype(BF16).reshape(per, block, HDIM)
            )
            return inner

        lax.fori_loop(0, tokens // QROWS, rows_step, 0)

    def spatial_step(j, carry):
        spatial(j)
        return carry

    pair_values(0).wait_recv()
    pair_keys(0).wait_recv()
    lax.fori_loop(0, 1, spatial_step, 0)
    for j in FLEX:
        wait_bytes(rcv.at[j, pl.ds(0, frames - 2)], fwd_recv.at[j - 1])
        temporal(j)

    wait_bytes(rcv.at[0, pl.ds(0, frames - 1), V], va_sems.at[1])
    wait_bytes(rcv.at[0, pl.ds(0, frames - 1), QK], qka_sems.at[1])
    temporal(0)
    lax.fori_loop(ND, NS, spatial_step, 0)
    pair_values(1).wait_recv()
    pair_keys(1).wait_recv()
    lax.fori_loop(1, 2, spatial_step, 0)

    for j in range(NT):
        wait_bytes(res.at[j, pl.ds(0, frames - 1)], ret_recv.at[j])
    for h in range(heads):
        total = None
        for slot in range(NT + NS):
            if fits(slot, h):
                term = res[slot].reshape(tokens, HDIM) * one_hot[slot, h]
                total = term if total is None else total + term
        out_ref[:, h * HDIM : (h + 1) * HDIM] = total

    wait_bytes(ss_all.at[pl.ds(0, groups - 1)], ss_sems.at[0])
    wait_bytes(snd.at[0, pl.ds(0, frames - 1), V], va_sems.at[0])
    wait_bytes(snd.at[0, pl.ds(0, frames - 1), QK], qka_sems.at[0])
    for j in range(NT):
        wait_bytes(ot.at[j, pl.ds(0, frames - 1)], ret_send.at[j])
    for j in FLEX:
        wait_bytes(out_msg.at[j - 1], out_send.at[j - 1])
        near_copy(j).wait_send()
        far_copy(j).wait_send()
        wait_bytes(rcv.at[j, pl.ds(0, frames - 2)], fwd_send.at[j - 1])
    for j in range(ND):
        pair_keys(j).wait_send()
        pair_values(j).wait_send()


def shards(query, key, value, gain_q, gain_k, head_kind):
    tokens, width = query.shape
    frames = lax.axis_size("ctx") // 2
    groups = lax.axis_size("head")
    block = tokens // frames
    vmem = pl.BlockSpec(memory_space=pltpu.VMEM)
    dma = pltpu.SemaphoreType.DMA
    return pl.pallas_call(
        functools.partial(kernel, frames, groups),
        out_shape=jax.ShapeDtypeStruct((tokens, width), BF16),
        in_specs=[pl.BlockSpec(memory_space=pltpu.SMEM)] + [vmem] * 5,
        out_specs=vmem,
        scratch_shapes=[
            pltpu.VMEM((NT, frames, 3 * block, HDIM), BF16),
            pltpu.VMEM((NT, frames, 3 * block, HDIM), BF16),
            pltpu.VMEM((NT, frames, block, HDIM), BF16),
            pltpu.VMEM((NT + NS, frames, block, HDIM), BF16),
            pltpu.VMEM((NS, 2 * tokens + PAD, HDIM), BF16),
            pltpu.VMEM((NS, 2 * tokens + PAD, HDIM), BF16),
            pltpu.VMEM((NS, tokens, HDIM), BF16),
            pltpu.VMEM((tokens, width), BF16),
            pltpu.VMEM((tokens, width), BF16),
            pltpu.VMEM((tokens, HDIM), F32),
            pltpu.VMEM((tokens, HDIM), F32),
            pltpu.VMEM((2, 8, CHUNK), F32),
            pltpu.VMEM((groups, 2, 8, CHUNK), F32),
            pltpu.VMEM((2, 18 * block, HDIM), BF16),
            pltpu.VMEM((2, 18 * block, HDIM), BF16),
            pltpu.VMEM((2, 18 * block, HDIM), BF16),
            dma((2,)), dma((2,)), dma((2,)), dma((NT,)), dma((NT,)), dma((2, ND)), dma((2, ND)),
            dma((2, 2)), dma((2,)), dma((2,)), dma((2, 2)), dma((2,)), dma((2,)),
        ],
        compiler_params=pltpu.CompilerParams(
            collective_id=0, has_side_effects=True, vmem_limit_bytes=56 * 2**20
        ),
        cost_estimate=pl.CostEstimate(
            flops=4 * NS * tokens * 2 * tokens * HDIM,
            bytes_accessed=8 * tokens * width,
            transcendentals=NS * 2 * tokens * tokens,
        ),
        name="head_attention",
    )(head_kind, query, key, value, gain_q, gain_k)


def solution(mesh):
    return jax.shard_map(
        shards,
        mesh=mesh,
        in_specs=(P("ctx", "head"), P("ctx", "head"), P("ctx", "head"), P("head"), P("head"), P()),
        out_specs=P("ctx", "head"),
        check_vma=False,
    )
```

```python
import functools
import math

import jax
import jax.numpy as jnp
from jax import lax
from jax.experimental import pallas as pl
from jax.experimental.pallas import tpu as pltpu
from jax.sharding import PartitionSpec as P

HEADS = 40
HDIM = 128
EPSILON = 1e-06
NT = 3
NS = 4
ND = 2
FLEX = (2, 1)
SPATIAL_OF = {2: 2, 1: 3}
MZ = 4
PAD = 256
CHUNK = 128
QROWS = 256
MESH = pl.DeviceIdType.MESH
BF16 = jnp.bfloat16
F32 = jnp.float32


def dot_nt(a, b):
    return lax.dot_general(a, b, (((1,), (1,)), ((), ())), preferred_element_type=F32)


def dot_nn(a, b):
    return lax.dot_general(a, b, (((1,), (0,)), ((), ())), preferred_element_type=F32)


def kernel(
    frames, groups, kind_ref, q_hbm, k_hbm, v_hbm, gq_ref, gk_ref, res,
    q_ref, k_ref, v_ref, load_sems, snd, rcv, ot, spat, own, par, qs, qn, kn, rq, rk, ss_own, ss_all, out_msg, near_msg, far_msg,
    ss_sems, va_sems, qka_sems, ret_send, ret_recv, k_sems, v_sems,
    near_sems, out_send, out_recv, far_sems, fwd_send, fwd_recv, self_sems, spat_sems,
):
    tokens, width = q_hbm.shape
    heads = width // HDIM
    block = tokens // frames
    chunks = tokens // CHUNK
    score_scale = 1.0 / math.sqrt(HDIM)
    ctx = lax.axis_index("ctx")
    group = lax.axis_index("head")
    frame, half = ctx // 2, ctx % 2
    y, m = frame // MZ, frame % MZ
    sign = 1 - 2 * half
    partner = ctx + 1 - 2 * half
    ny = frames // MZ

    def frame_at(dy, dm):
        return lax.rem(y + dy + ny, ny) * MZ + lax.rem(m + dm + MZ, MZ)

    def to_ctx(to_frame, to_half):
        return {"ctx": 2 * to_frame + to_half}

    in_frames = [frame_at(b, sign) for b in range(4)] + [frame_at(b, 2) for b in (0, 1)]
    out_frames = [frame_at(b, -sign) for b in range(4)] + [frame_at(b, 2) for b in (2, 3)]

    barrier = pltpu.get_barrier_semaphore()

    def greet(device_id):
        pl.semaphore_signal(barrier, inc=1, device_id=device_id, device_id_type=MESH)

    def peer_of(d):
        return lax.rem(frame + d, frames)

    def greet_ctx(d, carry):
        greet(to_ctx(peer_of(d), half))
        return carry

    def greet_head(d, carry):
        greet({"head": lax.rem(group + d, groups)})
        return carry

    loads = [
        pltpu.make_async_copy(src, dst, load_sems.at[n])
        for n, (src, dst) in enumerate(((v_hbm, v_ref), (q_hbm, q_ref), (k_hbm, k_ref)))
    ]
    for load in loads:
        load.start()

    greet({"ctx": partner})
    for b in range(4):
        greet(to_ctx(frame_at(b, -sign), 1 - half))
    for b in (0, 1, 3):
        greet(to_ctx(frame_at(b, 2), 1 - half))
    lax.fori_loop(1, frames, greet_ctx, 0)
    lax.fori_loop(1, groups, greet_head, 0)

    one_hot = {}
    seen = jnp.zeros((1, HDIM), jnp.int32)
    for h in range(heads):
        kind = jnp.full((1, HDIM), kind_ref[group * heads + h], jnp.int32)
        for slot in range(NT + NS):
            if slot < NT:
                chosen = (kind == 1) & (seen == slot)
            else:
                chosen = (kind == 0) & (h - seen == slot - NT)
            one_hot[slot, h] = jnp.where(chosen, 1.0, 0.0).astype(BF16)
        seen = seen + kind

    def fits(slot, h):
        if slot < NT:
            return h >= slot
        return 0 <= h - (slot - NT) <= NT

    def pick(ref, slot):
        total = None
        for h in range(heads):
            if fits(slot, h):
                term = ref[:, h * HDIM : (h + 1) * HDIM] * one_hot[slot, h]
                total = term if total is None else total + term
        return total

    V, Q, K = (pl.ds(n * block, block) for n in range(3))
    KEYS, VALUES = pl.ds(0, tokens), pl.ds(tokens, tokens)

    def blocks_of(x):
        return x.reshape(frames, block, HDIM)

    def remote(src, dst, send, recv, device_id):
        return pltpu.make_async_remote_copy(
            src_ref=src, dst_ref=dst, send_sem=send, recv_sem=recv,
            device_id=device_id, device_id_type=MESH,
        )

    def wait_bytes(ref, sem):
        pltpu.make_async_copy(ref, ref, sem).wait()

    def pair_keys(j):
        return remote(own.at[j, KEYS], par.at[j, KEYS], k_sems.at[0, j], k_sems.at[1, j], {"ctx": partner})

    def pair_values(j):
        return remote(own.at[j, VALUES], par.at[j, VALUES], v_sems.at[0, j], v_sems.at[1, j], {"ctx": partner})

    loads[0].wait()
    snd[0, :, V, :] = blocks_of(pick(v_ref, 0))

    pl.semaphore_wait(barrier, frames - 1 + groups - 1 + 8)

    def send_va(d, carry):
        to = peer_of(d)
        remote(
            snd.at[0, to, V], rcv.at[0, frame, V], va_sems.at[0], va_sems.at[1], to_ctx(to, half)
        ).start()
        return carry

    lax.fori_loop(1, frames, send_va, 0)
    for j in (0,):
        own[j, VALUES, :] = pick(v_ref, NT + j)
        pair_values(j).start()

    sub = lax.broadcasted_iota(jnp.int32, (8, CHUNK), 0)

    def squares(i, carry):
        rows = pl.ds(pl.multiple_of(i * CHUNK, CHUNK), CHUNK)
        kept = []
        for ref, tile in ((q_ref, carry[0]), (k_ref, carry[1])):
            part = ref[rows, :].astype(F32)
            total = jnp.sum(part * part, axis=1, keepdims=True)
            row = jnp.broadcast_to(total, (CHUNK, CHUNK)).T[0:8]
            kept.append(jnp.where(sub == i, row, tile))
        return tuple(kept)

    loads[1].wait()
    loads[2].wait()
    zero = jnp.zeros((8, CHUNK), F32)
    tiles = lax.fori_loop(0, chunks, squares, (zero, zero))
    for n in range(2):
        ss_own[n] = tiles[n]
        ss_all[group, n] = tiles[n]

    def send_squares(d, carry):
        remote(
            ss_own, ss_all.at[group], ss_sems.at[0], ss_sems.at[1],
            {"head": lax.rem(group + d, groups)},
        ).start()
        return carry

    lax.fori_loop(1, groups, send_squares, 0)

    for j in FLEX:
        snd[j, :, V, :] = blocks_of(pick(v_ref, j))
        own[SPATIAL_OF[j], VALUES, :] = pick(v_ref, NT + SPATIAL_OF[j])
        own[SPATIAL_OF[j], pl.ds(2 * tokens, PAD), :] = jnp.zeros((PAD, HDIM), BF16)

    wait_bytes(ss_all.at[pl.ds(0, groups - 1)], ss_sems.at[1])
    for n, column in ((0, rq), (1, rk)):
        total = ss_all[0, n]
        for g in range(1, groups):
            total = total + ss_all[g, n]
        inverse = lax.rsqrt(total * (1.0 / (HEADS * HDIM)) + EPSILON)
        for i in range(chunks):
            column[pl.ds(i * CHUNK, CHUNK), :] = jnp.broadcast_to(
                inverse[i : i + 1, :], (CHUNK, CHUNK)
            ).T

    for h in range(heads):
        at = slice(h * HDIM, (h + 1) * HDIM)
        qn[:, at] = (q_ref[:, at].astype(F32) * rq[...] * gq_ref[at]).astype(BF16)
        kn[:, at] = (k_ref[:, at].astype(F32) * rk[...] * gk_ref[at]).astype(BF16)

    size = 3 * block

    def near_copy(j):
        s = SPATIAL_OF[j]
        return remote(
            near_msg.at[j - 1], par.at[s, pl.ds(0, 6 * size)],
            near_sems.at[0, j - 1], near_sems.at[1, j - 1], {"ctx": partner},
        )

    def far_copy(j):
        s = SPATIAL_OF[j]
        return remote(
            far_msg.at[j - 1], par.at[s, pl.ds(6 * size, 6 * size)],
            far_sems.at[0, j - 1], far_sems.at[1, j - 1], {"ctx": partner},
        )

    for j in FLEX:
        s = SPATIAL_OF[j]
        snd[j, :, Q, :] = blocks_of(pick(qn, j))
        snd[j, :, K, :] = blocks_of(pick(kn, j))
        for b in range(6):
            remote(
                snd.at[j, out_frames[b]], out_msg.at[j - 1, pl.ds(b * size, size)],
                out_send.at[j - 1], out_recv.at[j - 1], to_ctx(frame_at(0, -sign), 1 - half),
            ).start()
        own[s, KEYS, :] = pick(kn, NT + s)
        for b in range(6):
            near_msg[j - 1, pl.ds(b * size, size), :] = (
                snd[j, in_frames[b]] + own[s, pl.ds(b * size, size), :]
            )
        near_copy(j).start()
        for b in range(1, 4):
            remote(
                snd.at[j, frame_at(b, 0)], rcv.at[j, frame],
                fwd_send.at[j - 1], fwd_recv.at[j - 1], to_ctx(frame_at(b, 0), half),
            ).start()
        rcv[j, frame] = snd[j, frame]
        qs[s] = pick(qn, NT + s)

    for j in (0,):
        own[j, KEYS, :] = pick(kn, NT + j)
        pair_keys(j).start()
        qs[j] = pick(qn, NT + j)

    for j in FLEX:
        s = SPATIAL_OF[j]
        wait_bytes(out_msg.at[j - 1], out_recv.at[j - 1])
        for b in range(6):
            at = pl.ds(b * size, size)
            far_msg[j - 1, at, :] = out_msg[j - 1, at, :] + own[s, pl.ds((6 + b) * size, size), :]
        far_copy(j).start()

    for j in FLEX:
        s = SPATIAL_OF[j]
        near_copy(j).wait_recv()
        for b in range(6):
            to = frame_at(b, -sign) if b < 4 else frame_at(b - 4, 2)
            remote(
                par.at[s, pl.ds(b * size, size)], rcv.at[j, frame],
                fwd_send.at[j - 1], fwd_recv.at[j - 1], to_ctx(to, 1 - half),
            ).start()
    for j in (1,):
        own[j, VALUES, :] = pick(v_ref, NT + j)
        pair_values(j).start()
    for j in FLEX:
        s = SPATIAL_OF[j]
        far_copy(j).wait_recv()
        origin = frame_at(0, sign)
        for b in range(1, 6):
            to = frame_at(b, 0) if b < 4 else frame_at(b - 2, -sign)
            remote(
                par.at[s, pl.ds((6 + b) * size, size)], rcv.at[j, origin],
                fwd_send.at[j - 1], fwd_recv.at[j - 1], to_ctx(to, half),
            ).start()
        rcv[j, origin] = par[s, pl.ds(6 * size, size), :]

    snd[0, :, Q, :] = blocks_of(pick(qn, 0))
    snd[0, :, K, :] = blocks_of(pick(kn, 0))
    QK = pl.ds(block, 2 * block)

    def send_qka(d, carry):
        to = peer_of(d)
        remote(
            snd.at[0, to, QK], rcv.at[0, frame, QK], qka_sems.at[0], qka_sems.at[1], to_ctx(to, half)
        ).start()
        return carry

    lax.fori_loop(1, frames, send_qka, 0)
    rcv[0, frame] = snd[0, frame]

    for j in (1,):
        own[j, KEYS, :] = pick(kn, NT + j)
        pair_keys(j).start()
        qs[j] = pick(qn, NT + j)

    step_rows = 16 * frames
    same = (
        lax.rem(lax.broadcasted_iota(jnp.int32, (step_rows, step_rows), 0), 16)
        == lax.rem(lax.broadcasted_iota(jnp.int32, (step_rows, step_rows), 1), 16)
    )

    def temporal(j):
        def rows(n, c):
            return rcv[j, :, pl.ds(n * block + c * 16, 16), :].reshape(step_rows, HDIM)

        for c in range(block // 16):
            value, query, key = rows(0, c), rows(1, c), rows(2, c)
            scores = jnp.where(same, dot_nt(query, key) * score_scale, -jnp.inf)
            expo = jnp.exp(scores - jnp.max(scores, axis=1, keepdims=True))
            weights = (expo / jnp.sum(expo, axis=1, keepdims=True)).astype(BF16)
            mixed = dot_nn(weights, value).astype(BF16)
            ot[j, :, pl.ds(c * 16, 16), :] = mixed.reshape(frames, 16, HDIM)

        def send_ret(d, carry):
            to = peer_of(d)
            remote(
                ot.at[j, to], res.at[j, frame], ret_send.at[j], ret_recv.at[j], to_ctx(to, half)
            ).start()
            return carry

        lax.fori_loop(1, frames, send_ret, 0)
        pltpu.make_async_copy(ot.at[j, frame], res.at[j, frame], self_sems.at[j]).start()

    def store_spatial(j):
        return pltpu.make_async_copy(spat.at[j], res.at[NT + j], spat_sems.at[j])

    def spatial(j):
        own_key, own_value, par_key, par_value = own[j, KEYS], own[j, VALUES], par[j, KEYS], par[j, VALUES]

        def rows_step(i, inner):
            query = qs[j, pl.ds(pl.multiple_of(i * QROWS, QROWS), QROWS), :]
            s_own = dot_nt(query, own_key) * score_scale
            s_par = dot_nt(query, par_key) * score_scale
            top = jnp.maximum(
                jnp.max(s_own, axis=1, keepdims=True), jnp.max(s_par, axis=1, keepdims=True)
            )
            e_own = jnp.exp(s_own - top)
            e_par = jnp.exp(s_par - top)
            total = jnp.sum(e_own, axis=1, keepdims=True) + jnp.sum(e_par, axis=1, keepdims=True)
            mixed = dot_nn(e_own.astype(BF16), own_value) + dot_nn(e_par.astype(BF16), par_value)
            per = QROWS // block
            spat[j, pl.ds(i * per, per)] = (
                (mixed / total).astype(BF16).reshape(per, block, HDIM)
            )
            return inner

        lax.fori_loop(0, tokens // QROWS, rows_step, 0)
        store_spatial(j).start()

    def spatial_step(j, carry):
        spatial(j)
        return carry

    pair_values(0).wait_recv()
    pair_keys(0).wait_recv()
    lax.fori_loop(0, 1, spatial_step, 0)
    for j in FLEX:
        wait_bytes(rcv.at[j, pl.ds(0, frames - 2)], fwd_recv.at[j - 1])
        temporal(j)

    wait_bytes(rcv.at[0, pl.ds(0, frames - 1), V], va_sems.at[1])
    wait_bytes(rcv.at[0, pl.ds(0, frames - 1), QK], qka_sems.at[1])
    temporal(0)
    lax.fori_loop(ND, NS, spatial_step, 0)
    pair_values(1).wait_recv()
    pair_keys(1).wait_recv()
    lax.fori_loop(1, 2, spatial_step, 0)

    for j in range(NT):
        wait_bytes(res.at[j, pl.ds(0, frames - 1)], ret_recv.at[j])
    for j in range(NT):
        pltpu.make_async_copy(ot.at[j, frame], res.at[j, frame], self_sems.at[j]).wait()
    for j in range(NS):
        store_spatial(j).wait()
    wait_bytes(ss_all.at[pl.ds(0, groups - 1)], ss_sems.at[0])
    wait_bytes(snd.at[0, pl.ds(0, frames - 1), V], va_sems.at[0])
    wait_bytes(snd.at[0, pl.ds(0, frames - 1), QK], qka_sems.at[0])
    for j in range(NT):
        wait_bytes(ot.at[j, pl.ds(0, frames - 1)], ret_send.at[j])
    for j in FLEX:
        wait_bytes(out_msg.at[j - 1], out_send.at[j - 1])
        near_copy(j).wait_send()
        far_copy(j).wait_send()
        wait_bytes(rcv.at[j, pl.ds(0, frames - 2)], fwd_send.at[j - 1])
    for j in range(ND):
        pair_keys(j).wait_send()
        pair_values(j).wait_send()


def gather_heads(kind_ref, slots_ref, out_ref, held, sems):
    heads = out_ref.shape[1] // HDIM
    first = lax.axis_index("head") * heads
    loads, stores = [], []
    seen = jnp.int32(0)
    for h in range(heads):
        is_temporal = kind_ref[first + h] == 1
        slot = jnp.where(is_temporal, seen, NT + h - seen)
        seen = seen + kind_ref[first + h]
        loads.append(pltpu.make_async_copy(slots_ref.at[slot], held.at[h], sems.at[0, h]))
        stores.append(
            pltpu.make_async_copy(held.at[h], out_ref.at[:, pl.ds(h * HDIM, HDIM)], sems.at[1, h])
        )
        loads[-1].start()
    for load, store in zip(loads, stores):
        load.wait()
        store.start()
    for store in stores:
        store.wait()


def shards(query, key, value, gain_q, gain_k, head_kind):
    tokens, width = query.shape
    frames = lax.axis_size("ctx") // 2
    groups = lax.axis_size("head")
    block = tokens // frames
    vmem = pl.BlockSpec(memory_space=pltpu.VMEM)
    dma = pltpu.SemaphoreType.DMA
    slots = pl.pallas_call(
        functools.partial(kernel, frames, groups),
        out_shape=jax.ShapeDtypeStruct((NT + NS, frames, block, HDIM), BF16),
        in_specs=[pl.BlockSpec(memory_space=pltpu.SMEM)] + [pl.BlockSpec(memory_space=pl.ANY)] * 3 + [vmem] * 2,
        out_specs=pl.BlockSpec(memory_space=pl.ANY),
        scratch_shapes=[
            pltpu.VMEM((tokens, width), BF16),
            pltpu.VMEM((tokens, width), BF16),
            pltpu.VMEM((tokens, width), BF16),
            dma((3,)),
            pltpu.VMEM((NT, frames, 3 * block, HDIM), BF16),
            pltpu.VMEM((NT, frames, 3 * block, HDIM), BF16),
            pltpu.VMEM((NT, frames, block, HDIM), BF16),
            pltpu.VMEM((NS, frames, block, HDIM), BF16),
            pltpu.VMEM((NS, 2 * tokens + PAD, HDIM), BF16),
            pltpu.VMEM((NS, 2 * tokens + PAD, HDIM), BF16),
            pltpu.VMEM((NS, tokens, HDIM), BF16),
            pltpu.VMEM((tokens, width), BF16),
            pltpu.VMEM((tokens, width), BF16),
            pltpu.VMEM((tokens, HDIM), F32),
            pltpu.VMEM((tokens, HDIM), F32),
            pltpu.VMEM((2, 8, CHUNK), F32),
            pltpu.VMEM((groups, 2, 8, CHUNK), F32),
            pltpu.VMEM((2, 18 * block, HDIM), BF16),
            pltpu.VMEM((2, 18 * block, HDIM), BF16),
            pltpu.VMEM((2, 18 * block, HDIM), BF16),
            dma((2,)), dma((2,)), dma((2,)), dma((NT,)), dma((NT,)), dma((2, ND)), dma((2, ND)),
            dma((2, 2)), dma((2,)), dma((2,)), dma((2, 2)), dma((2,)), dma((2,)), dma((NT,)), dma((NS,)),
        ],
        compiler_params=pltpu.CompilerParams(
            collective_id=0, has_side_effects=True, vmem_limit_bytes=56 * 2**20
        ),
        cost_estimate=pl.CostEstimate(
            flops=4 * NS * tokens * 2 * tokens * HDIM,
            bytes_accessed=8 * tokens * width,
            transcendentals=NS * 2 * tokens * tokens,
        ),
        name="head_attention",
    )(head_kind, query, key, value, gain_q, gain_k)
    return pl.pallas_call(
        gather_heads,
        out_shape=jax.ShapeDtypeStruct((tokens, width), BF16),
        in_specs=[pl.BlockSpec(memory_space=pltpu.SMEM), pl.BlockSpec(memory_space=pl.ANY)],
        out_specs=pl.BlockSpec(memory_space=pl.ANY),
        scratch_shapes=[pltpu.VMEM((width // HDIM, tokens, HDIM), BF16), dma((2, width // HDIM))],
        name="gather_heads",
    )(head_kind, slots.reshape(NT + NS, tokens, HDIM))


def solution(mesh):
    return jax.shard_map(
        shards,
        mesh=mesh,
        in_specs=(P("ctx", "head"), P("ctx", "head"), P("ctx", "head"), P("head"), P("head"), P()),
        out_specs=P("ctx", "head"),
        check_vma=False,
    )
```

```python
import functools
import math

import jax
import jax.numpy as jnp
from jax import lax
from jax.experimental import pallas as pl
from jax.experimental.pallas import tpu as pltpu
from jax.sharding import PartitionSpec as P

HEADS = 40
HDIM = 128
EPSILON = 1e-06
NT = 3
NS = 4
ND = 2
FLEX = (2, 1)
SPATIAL_OF = {2: 2, 1: 3}
MZ = 4
PAD = 256
CHUNK = 128
QROWS = 256
MESH = pl.DeviceIdType.MESH
BF16 = jnp.bfloat16
F32 = jnp.float32


def dot_nt(a, b):
    return lax.dot_general(a, b, (((1,), (1,)), ((), ())), preferred_element_type=F32)


def dot_nn(a, b):
    return lax.dot_general(a, b, (((1,), (0,)), ((), ())), preferred_element_type=F32)


def kernel(
    frames, groups, kind_hbm, q_hbm, k_hbm, v_hbm, gq_hbm, gk_hbm, res,
    kind_ref, gq_ref, gk_ref, q_ref, k_ref, v_ref, load_sems, snd, rcv, ot, spat, own, par, qs, qn, kn, rq, rk, ss_own, ss_all, out_msg, near_msg, far_msg,
    ss_sems, va_sems, qka_sems, ret_send, ret_recv, k_sems, v_sems,
    near_sems, out_send, out_recv, far_sems, fwd_send, fwd_recv, self_sems, spat_sems,
):
    tokens, width = q_hbm.shape
    heads = width // HDIM
    block = tokens // frames
    chunks = tokens // CHUNK
    score_scale = 1.0 / math.sqrt(HDIM)
    ctx = lax.axis_index("ctx")
    group = lax.axis_index("head")
    frame, half = ctx // 2, ctx % 2
    y, m = frame // MZ, frame % MZ
    sign = 1 - 2 * half
    partner = ctx + 1 - 2 * half
    ny = frames // MZ

    def frame_at(dy, dm):
        return lax.rem(y + dy + ny, ny) * MZ + lax.rem(m + dm + MZ, MZ)

    def to_ctx(to_frame, to_half):
        return {"ctx": 2 * to_frame + to_half}

    in_frames = [frame_at(b, sign) for b in range(4)] + [frame_at(b, 2) for b in (0, 1)]
    out_frames = [frame_at(b, -sign) for b in range(4)] + [frame_at(b, 2) for b in (2, 3)]

    barrier = pltpu.get_barrier_semaphore()

    def greet(device_id):
        pl.semaphore_signal(barrier, inc=1, device_id=device_id, device_id_type=MESH)

    def peer_of(d):
        return lax.rem(frame + d, frames)

    def greet_ctx(d, carry):
        greet(to_ctx(peer_of(d), half))
        return carry

    def greet_head(d, carry):
        greet({"head": lax.rem(group + d, groups)})
        return carry

    loads = [
        pltpu.make_async_copy(src, dst, load_sems.at[n])
        for n, (src, dst) in enumerate((
            (v_hbm, v_ref), (q_hbm, q_ref), (k_hbm, k_ref),
            (gq_hbm, gq_ref), (gk_hbm, gk_ref), (kind_hbm, kind_ref),
        ))
    ]
    for n in (5, 0, 1, 2, 3, 4):
        loads[n].start()

    greet({"ctx": partner})
    for b in range(4):
        greet(to_ctx(frame_at(b, -sign), 1 - half))
    for b in (0, 1, 3):
        greet(to_ctx(frame_at(b, 2), 1 - half))
    lax.fori_loop(1, frames, greet_ctx, 0)
    lax.fori_loop(1, groups, greet_head, 0)

    loads[5].wait()
    one_hot = {}
    seen = jnp.zeros((1, HDIM), jnp.int32)
    for h in range(heads):
        kind = jnp.full((1, HDIM), kind_ref[group * heads + h], jnp.int32)
        for slot in range(NT + NS):
            if slot < NT:
                chosen = (kind == 1) & (seen == slot)
            else:
                chosen = (kind == 0) & (h - seen == slot - NT)
            one_hot[slot, h] = jnp.where(chosen, 1.0, 0.0).astype(BF16)
        seen = seen + kind

    def fits(slot, h):
        if slot < NT:
            return h >= slot
        return 0 <= h - (slot - NT) <= NT

    def pick(ref, slot):
        total = None
        for h in range(heads):
            if fits(slot, h):
                term = ref[:, h * HDIM : (h + 1) * HDIM] * one_hot[slot, h]
                total = term if total is None else total + term
        return total

    V, Q, K = (pl.ds(n * block, block) for n in range(3))
    KEYS, VALUES = pl.ds(0, tokens), pl.ds(tokens, tokens)

    def blocks_of(x):
        return x.reshape(frames, block, HDIM)

    def remote(src, dst, send, recv, device_id):
        return pltpu.make_async_remote_copy(
            src_ref=src, dst_ref=dst, send_sem=send, recv_sem=recv,
            device_id=device_id, device_id_type=MESH,
        )

    def wait_bytes(ref, sem):
        pltpu.make_async_copy(ref, ref, sem).wait()

    def pair_keys(j):
        return remote(own.at[j, KEYS], par.at[j, KEYS], k_sems.at[0, j], k_sems.at[1, j], {"ctx": partner})

    def pair_values(j):
        return remote(own.at[j, VALUES], par.at[j, VALUES], v_sems.at[0, j], v_sems.at[1, j], {"ctx": partner})

    loads[0].wait()
    snd[0, :, V, :] = blocks_of(pick(v_ref, 0))

    pl.semaphore_wait(barrier, frames - 1 + groups - 1 + 8)

    def send_va(d, carry):
        to = peer_of(d)
        remote(
            snd.at[0, to, V], rcv.at[0, frame, V], va_sems.at[0], va_sems.at[1], to_ctx(to, half)
        ).start()
        return carry

    lax.fori_loop(1, frames, send_va, 0)
    for j in (0,):
        own[j, VALUES, :] = pick(v_ref, NT + j)
        pair_values(j).start()

    sub = lax.broadcasted_iota(jnp.int32, (8, CHUNK), 0)

    def squares(i, carry):
        rows = pl.ds(pl.multiple_of(i * CHUNK, CHUNK), CHUNK)
        kept = []
        for ref, tile in ((q_ref, carry[0]), (k_ref, carry[1])):
            part = ref[rows, :].astype(F32)
            total = jnp.sum(part * part, axis=1, keepdims=True)
            row = jnp.broadcast_to(total, (CHUNK, CHUNK)).T[0:8]
            kept.append(jnp.where(sub == i, row, tile))
        return tuple(kept)

    loads[1].wait()
    for n in (2, 3, 4):
        loads[n].wait()
    zero = jnp.zeros((8, CHUNK), F32)
    tiles = lax.fori_loop(0, chunks, squares, (zero, zero))
    for n in range(2):
        ss_own[n] = tiles[n]
        ss_all[group, n] = tiles[n]

    def send_squares(d, carry):
        remote(
            ss_own, ss_all.at[group], ss_sems.at[0], ss_sems.at[1],
            {"head": lax.rem(group + d, groups)},
        ).start()
        return carry

    lax.fori_loop(1, groups, send_squares, 0)

    for j in FLEX:
        snd[j, :, V, :] = blocks_of(pick(v_ref, j))
        own[SPATIAL_OF[j], VALUES, :] = pick(v_ref, NT + SPATIAL_OF[j])
        own[SPATIAL_OF[j], pl.ds(2 * tokens, PAD), :] = jnp.zeros((PAD, HDIM), BF16)

    wait_bytes(ss_all.at[pl.ds(0, groups - 1)], ss_sems.at[1])
    for n, column in ((0, rq), (1, rk)):
        total = ss_all[0, n]
        for g in range(1, groups):
            total = total + ss_all[g, n]
        inverse = lax.rsqrt(total * (1.0 / (HEADS * HDIM)) + EPSILON)
        for i in range(chunks):
            column[pl.ds(i * CHUNK, CHUNK), :] = jnp.broadcast_to(
                inverse[i : i + 1, :], (CHUNK, CHUNK)
            ).T

    for h in range(heads):
        at = slice(h * HDIM, (h + 1) * HDIM)
        qn[:, at] = (q_ref[:, at].astype(F32) * rq[...] * gq_ref[at]).astype(BF16)
        kn[:, at] = (k_ref[:, at].astype(F32) * rk[...] * gk_ref[at]).astype(BF16)

    size = 3 * block

    def near_copy(j):
        s = SPATIAL_OF[j]
        return remote(
            near_msg.at[j - 1], par.at[s, pl.ds(0, 6 * size)],
            near_sems.at[0, j - 1], near_sems.at[1, j - 1], {"ctx": partner},
        )

    def far_copy(j):
        s = SPATIAL_OF[j]
        return remote(
            far_msg.at[j - 1], par.at[s, pl.ds(6 * size, 6 * size)],
            far_sems.at[0, j - 1], far_sems.at[1, j - 1], {"ctx": partner},
        )

    for j in FLEX:
        s = SPATIAL_OF[j]
        snd[j, :, Q, :] = blocks_of(pick(qn, j))
        snd[j, :, K, :] = blocks_of(pick(kn, j))
        for b in range(6):
            remote(
                snd.at[j, out_frames[b]], out_msg.at[j - 1, pl.ds(b * size, size)],
                out_send.at[j - 1], out_recv.at[j - 1], to_ctx(frame_at(0, -sign), 1 - half),
            ).start()
        own[s, KEYS, :] = pick(kn, NT + s)
        for b in range(6):
            near_msg[j - 1, pl.ds(b * size, size), :] = (
                snd[j, in_frames[b]] + own[s, pl.ds(b * size, size), :]
            )
        near_copy(j).start()
        for b in range(1, 4):
            remote(
                snd.at[j, frame_at(b, 0)], rcv.at[j, frame],
                fwd_send.at[j - 1], fwd_recv.at[j - 1], to_ctx(frame_at(b, 0), half),
            ).start()
        rcv[j, frame] = snd[j, frame]
        qs[s] = pick(qn, NT + s)

    for j in (0,):
        own[j, KEYS, :] = pick(kn, NT + j)
        pair_keys(j).start()
        qs[j] = pick(qn, NT + j)

    for j in FLEX:
        s = SPATIAL_OF[j]
        wait_bytes(out_msg.at[j - 1], out_recv.at[j - 1])
        for b in range(6):
            at = pl.ds(b * size, size)
            far_msg[j - 1, at, :] = out_msg[j - 1, at, :] + own[s, pl.ds((6 + b) * size, size), :]
        far_copy(j).start()

    for j in FLEX:
        s = SPATIAL_OF[j]
        near_copy(j).wait_recv()
        for b in range(6):
            to = frame_at(b, -sign) if b < 4 else frame_at(b - 4, 2)
            remote(
                par.at[s, pl.ds(b * size, size)], rcv.at[j, frame],
                fwd_send.at[j - 1], fwd_recv.at[j - 1], to_ctx(to, 1 - half),
            ).start()
    for j in (1,):
        own[j, VALUES, :] = pick(v_ref, NT + j)
        pair_values(j).start()
    for j in FLEX:
        s = SPATIAL_OF[j]
        far_copy(j).wait_recv()
        origin = frame_at(0, sign)
        for b in range(1, 6):
            to = frame_at(b, 0) if b < 4 else frame_at(b - 2, -sign)
            remote(
                par.at[s, pl.ds((6 + b) * size, size)], rcv.at[j, origin],
                fwd_send.at[j - 1], fwd_recv.at[j - 1], to_ctx(to, half),
            ).start()
        rcv[j, origin] = par[s, pl.ds(6 * size, size), :]

    snd[0, :, Q, :] = blocks_of(pick(qn, 0))
    snd[0, :, K, :] = blocks_of(pick(kn, 0))
    QK = pl.ds(block, 2 * block)

    def send_qka(d, carry):
        to = peer_of(d)
        remote(
            snd.at[0, to, QK], rcv.at[0, frame, QK], qka_sems.at[0], qka_sems.at[1], to_ctx(to, half)
        ).start()
        return carry

    lax.fori_loop(1, frames, send_qka, 0)
    rcv[0, frame] = snd[0, frame]

    for j in (1,):
        own[j, KEYS, :] = pick(kn, NT + j)
        pair_keys(j).start()
        qs[j] = pick(qn, NT + j)

    step_rows = 16 * frames
    same = (
        lax.rem(lax.broadcasted_iota(jnp.int32, (step_rows, step_rows), 0), 16)
        == lax.rem(lax.broadcasted_iota(jnp.int32, (step_rows, step_rows), 1), 16)
    )

    def temporal(j):
        def rows(n, c):
            return rcv[j, :, pl.ds(n * block + c * 16, 16), :].reshape(step_rows, HDIM)

        for c in range(block // 16):
            value, query, key = rows(0, c), rows(1, c), rows(2, c)
            scores = jnp.where(same, dot_nt(query, key) * score_scale, -jnp.inf)
            expo = jnp.exp(scores - jnp.max(scores, axis=1, keepdims=True))
            weights = (expo / jnp.sum(expo, axis=1, keepdims=True)).astype(BF16)
            mixed = dot_nn(weights, value).astype(BF16)
            ot[j, :, pl.ds(c * 16, 16), :] = mixed.reshape(frames, 16, HDIM)

        def send_ret(d, carry):
            to = peer_of(d)
            remote(
                ot.at[j, to], res.at[j, frame], ret_send.at[j], ret_recv.at[j], to_ctx(to, half)
            ).start()
            return carry

        lax.fori_loop(1, frames, send_ret, 0)
        pltpu.make_async_copy(ot.at[j, frame], res.at[j, frame], self_sems.at[j]).start()

    def store_spatial(j):
        return pltpu.make_async_copy(spat.at[j], res.at[NT + j], spat_sems.at[j])

    def spatial(j):
        own_key, own_value, par_key, par_value = own[j, KEYS], own[j, VALUES], par[j, KEYS], par[j, VALUES]

        def rows_step(i, inner):
            query = qs[j, pl.ds(pl.multiple_of(i * QROWS, QROWS), QROWS), :]
            s_own = dot_nt(query, own_key) * score_scale
            s_par = dot_nt(query, par_key) * score_scale
            top = jnp.maximum(
                jnp.max(s_own, axis=1, keepdims=True), jnp.max(s_par, axis=1, keepdims=True)
            )
            e_own = jnp.exp(s_own - top)
            e_par = jnp.exp(s_par - top)
            total = jnp.sum(e_own, axis=1, keepdims=True) + jnp.sum(e_par, axis=1, keepdims=True)
            mixed = dot_nn(e_own.astype(BF16), own_value) + dot_nn(e_par.astype(BF16), par_value)
            per = QROWS // block
            spat[j, pl.ds(i * per, per)] = (
                (mixed / total).astype(BF16).reshape(per, block, HDIM)
            )
            return inner

        lax.fori_loop(0, tokens // QROWS, rows_step, 0)
        store_spatial(j).start()

    def spatial_step(j, carry):
        spatial(j)
        return carry

    pair_values(0).wait_recv()
    pair_keys(0).wait_recv()
    lax.fori_loop(0, 1, spatial_step, 0)
    wait_bytes(rcv.at[0, pl.ds(0, frames - 1), V], va_sems.at[1])
    wait_bytes(rcv.at[0, pl.ds(0, frames - 1), QK], qka_sems.at[1])
    temporal(0)
    for j in FLEX:
        wait_bytes(rcv.at[j, pl.ds(0, frames - 2)], fwd_recv.at[j - 1])
        temporal(j)

    lax.fori_loop(ND, NS, spatial_step, 0)
    pair_values(1).wait_recv()
    pair_keys(1).wait_recv()
    lax.fori_loop(1, 2, spatial_step, 0)

    for j in range(NT):
        wait_bytes(res.at[j, pl.ds(0, frames - 1)], ret_recv.at[j])
    for j in range(NT):
        pltpu.make_async_copy(ot.at[j, frame], res.at[j, frame], self_sems.at[j]).wait()
    for j in range(NS):
        store_spatial(j).wait()
    wait_bytes(ss_all.at[pl.ds(0, groups - 1)], ss_sems.at[0])
    wait_bytes(snd.at[0, pl.ds(0, frames - 1), V], va_sems.at[0])
    wait_bytes(snd.at[0, pl.ds(0, frames - 1), QK], qka_sems.at[0])
    for j in range(NT):
        wait_bytes(ot.at[j, pl.ds(0, frames - 1)], ret_send.at[j])
    for j in FLEX:
        wait_bytes(out_msg.at[j - 1], out_send.at[j - 1])
        near_copy(j).wait_send()
        far_copy(j).wait_send()
        wait_bytes(rcv.at[j, pl.ds(0, frames - 2)], fwd_send.at[j - 1])
    for j in range(ND):
        pair_keys(j).wait_send()
        pair_values(j).wait_send()


def gather_heads(kind_ref, slots_ref, out_ref, held, sems):
    heads = out_ref.shape[1] // HDIM
    first = lax.axis_index("head") * heads
    loads, stores = [], []
    seen = jnp.int32(0)
    for h in range(heads):
        is_temporal = kind_ref[first + h] == 1
        slot = jnp.where(is_temporal, seen, NT + h - seen)
        seen = seen + kind_ref[first + h]
        loads.append(pltpu.make_async_copy(slots_ref.at[slot], held.at[h], sems.at[0, h]))
        stores.append(
            pltpu.make_async_copy(held.at[h], out_ref.at[:, pl.ds(h * HDIM, HDIM)], sems.at[1, h])
        )
        loads[-1].start()
    for load, store in zip(loads, stores):
        load.wait()
        store.start()
    for store in stores:
        store.wait()


def shards(query, key, value, gain_q, gain_k, head_kind):
    tokens, width = query.shape
    frames = lax.axis_size("ctx") // 2
    groups = lax.axis_size("head")
    block = tokens // frames
    dma = pltpu.SemaphoreType.DMA
    slots = pl.pallas_call(
        functools.partial(kernel, frames, groups),
        out_shape=jax.ShapeDtypeStruct((NT + NS, frames, block, HDIM), BF16),
        in_specs=[pl.BlockSpec(memory_space=pl.ANY)] * 6,
        out_specs=pl.BlockSpec(memory_space=pl.ANY),
        scratch_shapes=[
            pltpu.SMEM(head_kind.shape, jnp.int32),
            pltpu.VMEM((width,), F32),
            pltpu.VMEM((width,), F32),
            pltpu.VMEM((tokens, width), BF16),
            pltpu.VMEM((tokens, width), BF16),
            pltpu.VMEM((tokens, width), BF16),
            dma((6,)),
            pltpu.VMEM((NT, frames, 3 * block, HDIM), BF16),
            pltpu.VMEM((NT, frames, 3 * block, HDIM), BF16),
            pltpu.VMEM((NT, frames, block, HDIM), BF16),
            pltpu.VMEM((NS, frames, block, HDIM), BF16),
            pltpu.VMEM((NS, 2 * tokens + PAD, HDIM), BF16),
            pltpu.VMEM((NS, 2 * tokens + PAD, HDIM), BF16),
            pltpu.VMEM((NS, tokens, HDIM), BF16),
            pltpu.VMEM((tokens, width), BF16),
            pltpu.VMEM((tokens, width), BF16),
            pltpu.VMEM((tokens, HDIM), F32),
            pltpu.VMEM((tokens, HDIM), F32),
            pltpu.VMEM((2, 8, CHUNK), F32),
            pltpu.VMEM((groups, 2, 8, CHUNK), F32),
            pltpu.VMEM((2, 18 * block, HDIM), BF16),
            pltpu.VMEM((2, 18 * block, HDIM), BF16),
            pltpu.VMEM((2, 18 * block, HDIM), BF16),
            dma((2,)), dma((2,)), dma((2,)), dma((NT,)), dma((NT,)), dma((2, ND)), dma((2, ND)),
            dma((2, 2)), dma((2,)), dma((2,)), dma((2, 2)), dma((2,)), dma((2,)), dma((NT,)), dma((NS,)),
        ],
        compiler_params=pltpu.CompilerParams(
            collective_id=0, has_side_effects=True, vmem_limit_bytes=56 * 2**20
        ),
        cost_estimate=pl.CostEstimate(
            flops=4 * NS * tokens * 2 * tokens * HDIM,
            bytes_accessed=8 * tokens * width,
            transcendentals=NS * 2 * tokens * tokens,
        ),
        name="head_attention",
    )(head_kind, query, key, value, gain_q, gain_k)
    return pl.pallas_call(
        gather_heads,
        out_shape=jax.ShapeDtypeStruct((tokens, width), BF16),
        in_specs=[pl.BlockSpec(memory_space=pltpu.SMEM), pl.BlockSpec(memory_space=pl.ANY)],
        out_specs=pl.BlockSpec(memory_space=pl.ANY),
        scratch_shapes=[pltpu.VMEM((width // HDIM, tokens, HDIM), BF16), dma((2, width // HDIM))],
        name="gather_heads",
    )(head_kind, slots.reshape(NT + NS, tokens, HDIM))


def solution(mesh):
    return jax.shard_map(
        shards,
        mesh=mesh,
        in_specs=(P("ctx", "head"), P("ctx", "head"), P("ctx", "head"), P("head"), P("head"), P()),
        out_specs=P("ctx", "head"),
        check_vma=False,
    )
```

```python
import functools
import math

import jax
import jax.numpy as jnp
from jax import lax
from jax.experimental import pallas as pl
from jax.experimental.pallas import tpu as pltpu
from jax.sharding import PartitionSpec as P

HEADS = 40
HDIM = 128
EPSILON = 1e-06
NT = 3
NS = 4
ND = 2
FLEX = (2, 1)
SPATIAL_OF = {2: 2, 1: 3}
MZ = 4
PAD = 256
CHUNK = 128
QROWS = 256
MESH = pl.DeviceIdType.MESH
BF16 = jnp.bfloat16
F32 = jnp.float32


def dot_nt(a, b):
    return lax.dot_general(a, b, (((1,), (1,)), ((), ())), preferred_element_type=F32)


def dot_nn(a, b):
    return lax.dot_general(a, b, (((1,), (0,)), ((), ())), preferred_element_type=F32)


def kernel(
    frames, groups, kind_hbm, q_hbm, k_hbm, v_hbm, gq_hbm, gk_hbm, res,
    kind_ref, gq_ref, gk_ref, q_ref, k_ref, v_ref, load_sems, snd, rcv, ot, spat, own, par, qs, qn, kn, rq, rk, ss_own, ss_all, out_msg, near_msg, far_msg,
    ss_sems, va_sems, qka_sems, ret_send, ret_recv, k_sems, v_sems,
    near_sems, out_send, out_recv, far_sems, fwd_send, fwd_recv, self_sems, spat_sems,
):
    tokens, width = q_hbm.shape
    heads = width // HDIM
    block = tokens // frames
    chunks = tokens // CHUNK
    score_scale = 1.0 / math.sqrt(HDIM)
    ctx = lax.axis_index("ctx")
    group = lax.axis_index("head")
    frame, half = ctx // 2, ctx % 2
    y, m = frame // MZ, frame % MZ
    sign = 1 - 2 * half
    partner = ctx + 1 - 2 * half
    ny = frames // MZ

    def frame_at(dy, dm):
        return lax.rem(y + dy + ny, ny) * MZ + lax.rem(m + dm + MZ, MZ)

    def to_ctx(to_frame, to_half):
        return {"ctx": 2 * to_frame + to_half}

    in_frames = [frame_at(b, sign) for b in range(4)] + [frame_at(b, 2) for b in (0, 1)]
    out_frames = [frame_at(b, -sign) for b in range(4)] + [frame_at(b, 2) for b in (2, 3)]

    barrier = pltpu.get_barrier_semaphore()

    def greet(device_id):
        pl.semaphore_signal(barrier, inc=1, device_id=device_id, device_id_type=MESH)

    def peer_of(d):
        return lax.rem(frame + d, frames)

    def greet_ctx(d, carry):
        greet(to_ctx(peer_of(d), half))
        return carry

    def greet_head(d, carry):
        greet({"head": lax.rem(group + d, groups)})
        return carry

    loads = [
        pltpu.make_async_copy(src, dst, load_sems.at[n])
        for n, (src, dst) in enumerate((
            (v_hbm, v_ref), (q_hbm, q_ref), (k_hbm, k_ref),
            (gq_hbm, gq_ref), (gk_hbm, gk_ref), (kind_hbm, kind_ref),
        ))
    ]
    for n in (5, 0, 1, 2, 3, 4):
        loads[n].start()

    greet({"ctx": partner})
    for b in range(4):
        greet(to_ctx(frame_at(b, -sign), 1 - half))
    for b in (0, 1, 3):
        greet(to_ctx(frame_at(b, 2), 1 - half))
    lax.fori_loop(1, frames, greet_ctx, 0)
    lax.fori_loop(1, groups, greet_head, 0)

    loads[5].wait()
    one_hot = {}
    seen = jnp.zeros((1, HDIM), jnp.int32)
    for h in range(heads):
        kind = jnp.full((1, HDIM), kind_ref[group * heads + h], jnp.int32)
        for slot in range(NT + NS):
            if slot < NT:
                chosen = (kind == 1) & (seen == slot)
            else:
                chosen = (kind == 0) & (h - seen == slot - NT)
            one_hot[slot, h] = jnp.where(chosen, 1.0, 0.0).astype(BF16)
        seen = seen + kind

    def fits(slot, h):
        if slot < NT:
            return h >= slot
        return 0 <= h - (slot - NT) <= NT

    def pick(ref, slot):
        total = None
        for h in range(heads):
            if fits(slot, h):
                term = ref[:, h * HDIM : (h + 1) * HDIM] * one_hot[slot, h]
                total = term if total is None else total + term
        return total

    V, Q, K = (pl.ds(n * block, block) for n in range(3))
    KEYS, VALUES = pl.ds(0, tokens), pl.ds(tokens, tokens)

    def blocks_of(x):
        return x.reshape(frames, block, HDIM)

    def remote(src, dst, send, recv, device_id):
        return pltpu.make_async_remote_copy(
            src_ref=src, dst_ref=dst, send_sem=send, recv_sem=recv,
            device_id=device_id, device_id_type=MESH,
        )

    def wait_bytes(ref, sem):
        pltpu.make_async_copy(ref, ref, sem).wait()

    def pair_keys(j):
        return remote(own.at[j, KEYS], par.at[j, KEYS], k_sems.at[0, j], k_sems.at[1, j], {"ctx": partner})

    def pair_values(j):
        return remote(own.at[j, VALUES], par.at[j, VALUES], v_sems.at[0, j], v_sems.at[1, j], {"ctx": partner})

    loads[0].wait()
    snd[0, :, V, :] = blocks_of(pick(v_ref, 0))

    pl.semaphore_wait(barrier, frames - 1 + groups - 1 + 8)

    def send_va(d, carry):
        to = peer_of(d)
        remote(
            snd.at[0, to, V], rcv.at[0, frame, V], va_sems.at[0], va_sems.at[1], to_ctx(to, half)
        ).start()
        return carry

    lax.fori_loop(1, frames, send_va, 0)
    for j in (0,):
        own[j, VALUES, :] = pick(v_ref, NT + j)
        pair_values(j).start()

    sub = lax.broadcasted_iota(jnp.int32, (8, CHUNK), 0)

    def squares(i, carry):
        rows = pl.ds(pl.multiple_of(i * CHUNK, CHUNK), CHUNK)
        kept = []
        for ref, tile in ((q_ref, carry[0]), (k_ref, carry[1])):
            part = ref[rows, :].astype(F32)
            total = jnp.sum(part * part, axis=1, keepdims=True)
            row = jnp.broadcast_to(total, (CHUNK, CHUNK)).T[0:8]
            kept.append(jnp.where(sub == i, row, tile))
        return tuple(kept)

    loads[1].wait()
    for n in (2, 3, 4):
        loads[n].wait()
    zero = jnp.zeros((8, CHUNK), F32)
    tiles = lax.fori_loop(0, chunks, squares, (zero, zero))
    for n in range(2):
        ss_own[n] = tiles[n]
        ss_all[group, n] = tiles[n]

    def send_squares(d, carry):
        remote(
            ss_own, ss_all.at[group], ss_sems.at[0], ss_sems.at[1],
            {"head": lax.rem(group + d, groups)},
        ).start()
        return carry

    lax.fori_loop(1, groups, send_squares, 0)

    for j in FLEX:
        snd[j, :, V, :] = blocks_of(pick(v_ref, j))
        own[SPATIAL_OF[j], VALUES, :] = pick(v_ref, NT + SPATIAL_OF[j])
        own[SPATIAL_OF[j], pl.ds(2 * tokens, PAD), :] = jnp.zeros((PAD, HDIM), BF16)

    wait_bytes(ss_all.at[pl.ds(0, groups - 1)], ss_sems.at[1])
    for n, column in ((0, rq), (1, rk)):
        total = ss_all[0, n]
        for g in range(1, groups):
            total = total + ss_all[g, n]
        inverse = lax.rsqrt(total * (1.0 / (HEADS * HDIM)) + EPSILON)
        for i in range(chunks):
            column[pl.ds(i * CHUNK, CHUNK), :] = jnp.broadcast_to(
                inverse[i : i + 1, :], (CHUNK, CHUNK)
            ).T

    for h in range(heads):
        at = slice(h * HDIM, (h + 1) * HDIM)
        qn[:, at] = (q_ref[:, at].astype(F32) * rq[...] * gq_ref[at]).astype(BF16)
        kn[:, at] = (k_ref[:, at].astype(F32) * rk[...] * gk_ref[at]).astype(BF16)

    size = 3 * block

    def near_copy(j):
        s = SPATIAL_OF[j]
        return remote(
            near_msg.at[j - 1], par.at[s, pl.ds(0, 6 * size)],
            near_sems.at[0, j - 1], near_sems.at[1, j - 1], {"ctx": partner},
        )

    def far_copy(j):
        s = SPATIAL_OF[j]
        return remote(
            far_msg.at[j - 1], par.at[s, pl.ds(6 * size, 6 * size)],
            far_sems.at[0, j - 1], far_sems.at[1, j - 1], {"ctx": partner},
        )

    for j in FLEX:
        s = SPATIAL_OF[j]
        snd[j, :, Q, :] = blocks_of(pick(qn, j))
        snd[j, :, K, :] = blocks_of(pick(kn, j))
        for b in range(6):
            remote(
                snd.at[j, out_frames[b]], out_msg.at[j - 1, pl.ds(b * size, size)],
                out_send.at[j - 1], out_recv.at[j - 1], to_ctx(frame_at(0, -sign), 1 - half),
            ).start()
        own[s, KEYS, :] = pick(kn, NT + s)
        for b in range(6):
            near_msg[j - 1, pl.ds(b * size, size), :] = (
                snd[j, in_frames[b]] + own[s, pl.ds(b * size, size), :]
            )
        near_copy(j).start()
        for b in range(1, 4):
            remote(
                snd.at[j, frame_at(b, 0)], rcv.at[j, frame],
                fwd_send.at[j - 1], fwd_recv.at[j - 1], to_ctx(frame_at(b, 0), half),
            ).start()
        rcv[j, frame] = snd[j, frame]
        qs[s] = pick(qn, NT + s)

    for j in (0,):
        own[j, KEYS, :] = pick(kn, NT + j)
        pair_keys(j).start()
        qs[j] = pick(qn, NT + j)

    for j in FLEX:
        s = SPATIAL_OF[j]
        wait_bytes(out_msg.at[j - 1], out_recv.at[j - 1])
        for b in range(6):
            at = pl.ds(b * size, size)
            far_msg[j - 1, at, :] = out_msg[j - 1, at, :] + own[s, pl.ds((6 + b) * size, size), :]
        far_copy(j).start()

    for j in FLEX:
        s = SPATIAL_OF[j]
        near_copy(j).wait_recv()
        for b in range(6):
            to = frame_at(b, -sign) if b < 4 else frame_at(b - 4, 2)
            remote(
                par.at[s, pl.ds(b * size, size)], rcv.at[j, frame],
                fwd_send.at[j - 1], fwd_recv.at[j - 1], to_ctx(to, 1 - half),
            ).start()
    for j in (1,):
        own[j, VALUES, :] = pick(v_ref, NT + j)
        pair_values(j).start()
    for j in FLEX:
        s = SPATIAL_OF[j]
        far_copy(j).wait_recv()
        origin = frame_at(0, sign)
        for b in range(1, 6):
            to = frame_at(b, 0) if b < 4 else frame_at(b - 2, -sign)
            remote(
                par.at[s, pl.ds((6 + b) * size, size)], rcv.at[j, origin],
                fwd_send.at[j - 1], fwd_recv.at[j - 1], to_ctx(to, half),
            ).start()
        rcv[j, origin] = par[s, pl.ds(6 * size, size), :]

    snd[0, :, Q, :] = blocks_of(pick(qn, 0))
    snd[0, :, K, :] = blocks_of(pick(kn, 0))
    QK = pl.ds(block, 2 * block)

    def send_qka(d, carry):
        to = peer_of(d)
        remote(
            snd.at[0, to, QK], rcv.at[0, frame, QK], qka_sems.at[0], qka_sems.at[1], to_ctx(to, half)
        ).start()
        return carry

    lax.fori_loop(1, frames, send_qka, 0)
    rcv[0, frame] = snd[0, frame]

    for j in (1,):
        own[j, KEYS, :] = pick(kn, NT + j)
        pair_keys(j).start()
        qs[j] = pick(qn, NT + j)

    step_rows = 16 * frames
    same = (
        lax.rem(lax.broadcasted_iota(jnp.int32, (step_rows, step_rows), 0), 16)
        == lax.rem(lax.broadcasted_iota(jnp.int32, (step_rows, step_rows), 1), 16)
    )

    def temporal(j):
        def rows(n, c):
            return rcv[j, :, pl.ds(n * block + c * 16, 16), :].reshape(step_rows, HDIM)

        for c in range(block // 16):
            value, query, key = rows(0, c), rows(1, c), rows(2, c)
            scores = jnp.where(same, dot_nt(query, key) * score_scale, -jnp.inf)
            expo = jnp.exp(scores - jnp.max(scores, axis=1, keepdims=True))
            weights = (expo / jnp.sum(expo, axis=1, keepdims=True)).astype(BF16)
            mixed = dot_nn(weights, value).astype(BF16)
            ot[j, :, pl.ds(c * 16, 16), :] = mixed.reshape(frames, 16, HDIM)

        def send_ret(d, carry):
            to = peer_of(d)
            remote(
                ot.at[j, to], res.at[j, frame], ret_send.at[j], ret_recv.at[j], to_ctx(to, half)
            ).start()
            return carry

        lax.fori_loop(1, frames, send_ret, 0)
        pltpu.make_async_copy(ot.at[j, frame], res.at[j, frame], self_sems.at[j]).start()

    def store_spatial(j):
        return pltpu.make_async_copy(spat.at[j], res.at[NT + j], spat_sems.at[j])

    def spatial(j):
        own_key, own_value, par_key, par_value = own[j, KEYS], own[j, VALUES], par[j, KEYS], par[j, VALUES]

        def rows_step(i, inner):
            query = qs[j, pl.ds(pl.multiple_of(i * QROWS, QROWS), QROWS), :]
            s_own = dot_nt(query, own_key) * score_scale
            s_par = dot_nt(query, par_key) * score_scale
            top = jnp.maximum(
                jnp.max(s_own, axis=1, keepdims=True), jnp.max(s_par, axis=1, keepdims=True)
            )
            e_own = jnp.exp(s_own - top)
            e_par = jnp.exp(s_par - top)
            total = jnp.sum(e_own, axis=1, keepdims=True) + jnp.sum(e_par, axis=1, keepdims=True)
            mixed = dot_nn(e_own.astype(BF16), own_value) + dot_nn(e_par.astype(BF16), par_value)
            per = QROWS // block
            spat[j, pl.ds(i * per, per)] = (
                (mixed / total).astype(BF16).reshape(per, block, HDIM)
            )
            return inner

        lax.fori_loop(0, tokens // QROWS, rows_step, 0)
        store_spatial(j).start()

    def spatial_step(j, carry):
        spatial(j)
        return carry

    pair_values(0).wait_recv()
    pair_keys(0).wait_recv()
    lax.fori_loop(0, 1, spatial_step, 0)
    wait_bytes(rcv.at[0, pl.ds(0, frames - 1), V], va_sems.at[1])
    wait_bytes(rcv.at[0, pl.ds(0, frames - 1), QK], qka_sems.at[1])
    temporal(0)
    for j in FLEX:
        wait_bytes(rcv.at[j, pl.ds(0, frames - 2)], fwd_recv.at[j - 1])
        temporal(j)

    lax.fori_loop(ND, NS, spatial_step, 0)
    pair_values(1).wait_recv()
    pair_keys(1).wait_recv()
    lax.fori_loop(1, 2, spatial_step, 0)

    for j in range(NT):
        wait_bytes(res.at[j, pl.ds(0, frames - 1)], ret_recv.at[j])
    for j in range(NT):
        pltpu.make_async_copy(ot.at[j, frame], res.at[j, frame], self_sems.at[j]).wait()
    for j in range(NS):
        store_spatial(j).wait()
    wait_bytes(ss_all.at[pl.ds(0, groups - 1)], ss_sems.at[0])
    wait_bytes(snd.at[0, pl.ds(0, frames - 1), V], va_sems.at[0])
    wait_bytes(snd.at[0, pl.ds(0, frames - 1), QK], qka_sems.at[0])
    for j in range(NT):
        wait_bytes(ot.at[j, pl.ds(0, frames - 1)], ret_send.at[j])
    for j in FLEX:
        wait_bytes(out_msg.at[j - 1], out_send.at[j - 1])
        near_copy(j).wait_send()
        far_copy(j).wait_send()
        wait_bytes(rcv.at[j, pl.ds(0, frames - 2)], fwd_send.at[j - 1])
    for j in range(ND):
        pair_keys(j).wait_send()
        pair_values(j).wait_send()


def gather_heads(kind_hbm, slots_ref, out_ref, kind_ref, held, kind_sem, load_sems, store_sems):
    heads = out_ref.shape[1] // HDIM
    first = lax.axis_index("head") * heads
    kinds = pltpu.make_async_copy(kind_hbm, kind_ref, kind_sem)
    kinds.start()
    loads = [
        pltpu.make_async_copy(slots_ref.at[n], held.at[n], load_sems.at[n]) for n in range(NT + NS)
    ]
    for load in loads:
        load.start()
    kinds.wait()
    stores = []
    seen = jnp.int32(0)
    for h in range(heads):
        is_temporal = kind_ref[first + h] == 1
        slot = jnp.where(is_temporal, seen, NT + h - seen)
        seen = seen + kind_ref[first + h]
        stores.append(
            pltpu.make_async_copy(
                held.at[slot], out_ref.at[:, pl.ds(h * HDIM, HDIM)], store_sems.at[h]
            )
        )
    for load in loads:
        load.wait()
    for store in stores:
        store.start()
    for store in stores:
        store.wait()


def shards(query, key, value, gain_q, gain_k, head_kind):
    tokens, width = query.shape
    frames = lax.axis_size("ctx") // 2
    groups = lax.axis_size("head")
    block = tokens // frames
    dma = pltpu.SemaphoreType.DMA
    slots = pl.pallas_call(
        functools.partial(kernel, frames, groups),
        out_shape=jax.ShapeDtypeStruct((NT + NS, frames, block, HDIM), BF16),
        in_specs=[pl.BlockSpec(memory_space=pl.ANY)] * 6,
        out_specs=pl.BlockSpec(memory_space=pl.ANY),
        scratch_shapes=[
            pltpu.SMEM(head_kind.shape, jnp.int32),
            pltpu.VMEM((width,), F32),
            pltpu.VMEM((width,), F32),
            pltpu.VMEM((tokens, width), BF16),
            pltpu.VMEM((tokens, width), BF16),
            pltpu.VMEM((tokens, width), BF16),
            dma((6,)),
            pltpu.VMEM((NT, frames, 3 * block, HDIM), BF16),
            pltpu.VMEM((NT, frames, 3 * block, HDIM), BF16),
            pltpu.VMEM((NT, frames, block, HDIM), BF16),
            pltpu.VMEM((NS, frames, block, HDIM), BF16),
            pltpu.VMEM((NS, 2 * tokens + PAD, HDIM), BF16),
            pltpu.VMEM((NS, 2 * tokens + PAD, HDIM), BF16),
            pltpu.VMEM((NS, tokens, HDIM), BF16),
            pltpu.VMEM((tokens, width), BF16),
            pltpu.VMEM((tokens, width), BF16),
            pltpu.VMEM((tokens, HDIM), F32),
            pltpu.VMEM((tokens, HDIM), F32),
            pltpu.VMEM((2, 8, CHUNK), F32),
            pltpu.VMEM((groups, 2, 8, CHUNK), F32),
            pltpu.VMEM((2, 18 * block, HDIM), BF16),
            pltpu.VMEM((2, 18 * block, HDIM), BF16),
            pltpu.VMEM((2, 18 * block, HDIM), BF16),
            dma((2,)), dma((2,)), dma((2,)), dma((NT,)), dma((NT,)), dma((2, ND)), dma((2, ND)),
            dma((2, 2)), dma((2,)), dma((2,)), dma((2, 2)), dma((2,)), dma((2,)), dma((NT,)), dma((NS,)),
        ],
        compiler_params=pltpu.CompilerParams(
            collective_id=0, has_side_effects=True, vmem_limit_bytes=56 * 2**20
        ),
        cost_estimate=pl.CostEstimate(
            flops=4 * NS * tokens * 2 * tokens * HDIM,
            bytes_accessed=8 * tokens * width,
            transcendentals=NS * 2 * tokens * tokens,
        ),
        name="head_attention",
    )(head_kind, query, key, value, gain_q, gain_k)
    return pl.pallas_call(
        gather_heads,
        out_shape=jax.ShapeDtypeStruct((tokens, width), BF16),
        in_specs=[pl.BlockSpec(memory_space=pl.ANY)] * 2,
        out_specs=pl.BlockSpec(memory_space=pl.ANY),
        scratch_shapes=[
            pltpu.SMEM(head_kind.shape, jnp.int32),
            pltpu.VMEM((NT + NS, tokens, HDIM), BF16),
            dma, dma((NT + NS,)), dma((width // HDIM,)),
        ],
        name="gather_heads",
    )(head_kind, slots.reshape(NT + NS, tokens, HDIM))


def solution(mesh):
    return jax.shard_map(
        shards,
        mesh=mesh,
        in_specs=(P("ctx", "head"), P("ctx", "head"), P("ctx", "head"), P("head"), P("head"), P()),
        out_specs=P("ctx", "head"),
        check_vma=False,
    )
```
